32 devices in a mesh: grp: 8 (over z, y), blk: 4 (over x, core).
Axes of the slice: x: 2, y: 2, z: 4, core: 2. Of those that a mesh axis runs over, the one named last changes fastest.
Arguments:
- source: bfloat16 [32768, 256], P(('grp', 'blk')), may hold values from -6 to 6
- send_ids: int32 [32, 8], P(('grp', 'blk')), may hold values from 0 to 15
- send_counts: int32 [32, 4], P(('grp', 'blk')), may hold values from 1 to 2, as said below
- tile_slot: int32 [32, 128], P(('grp', 'blk')), may hold values from 0 to 7, as said below
- tile_target: int32 [32, 128], P(('grp', 'blk')), may hold values from 0 to 63, as said below
- tile_weights: bfloat16 [4096, 4096], P(('grp', 'blk')), may hold values from 0 to 0.0625
Outputs:
- remapped: float32 [65536, 256], P(('grp', 'blk'))
The draws below stay inside these ranges and needn't reach their ends.
Inputs may be any that keep to these rules, and one draw needn't show every extreme that they name: `send_counts`: every reader of every partition is sent at least one block, and each partition sends 2 blocks to some reader. `tile_slot`: each of the 4 * 2 receive slots is read by at least one tile of every partition. `tile_target`: each of the 64 partial target blocks is written by at least one tile of every partition.
All inputs are finite; a program needn't handle non-finite values.
Results may differ from the reference program's by a relative error of at most 0.0003.
Values may be sent and summed in bfloat16 or wider, within the bound.
No kernel may reach another device: no remote copies, remote signals or barrier semaphores. Data moves between devices by JAX's collectives and lax.ppermute only.
A program may use at most 64 MiB of HBM per device.

```python
from functools import partial
import jax
import jax.numpy as jnp
from jax import lax

COLS = 256
BLOCK = 64
SB = 16
CAP = 2
TB = 32
EB = 16
NT = 128
PARTITIONS = 32
N_BLK = 4


def tile_lists(key):
    base_key = jax.random.fold_in(key, 17)
    target_key, slot_key, order_key = jax.random.split(base_key, 3)
    segments = TB + 2 * EB
    slot_total = N_BLK * CAP
    extra_targets = jax.random.randint(target_key, (PARTITIONS, NT - segments), 0, segments, dtype=jnp.int32)
    targets = jnp.concatenate([jnp.broadcast_to(jnp.arange(segments, dtype=jnp.int32)[None, :], (PARTITIONS, segments)), extra_targets], axis=1)
    extra_slots = jax.random.randint(slot_key, (PARTITIONS, NT - slot_total), 0, slot_total, dtype=jnp.int32)
    slots_all = jnp.concatenate([jnp.broadcast_to(jnp.arange(slot_total, dtype=jnp.int32)[None, :], (PARTITIONS, slot_total)), extra_slots], axis=1)
    row_keys = jax.random.split(order_key, PARTITIONS)
    orders = jax.vmap(lambda row_key: jax.random.permutation(row_key, NT))(row_keys).astype(jnp.int32)
    return (jnp.take_along_axis(targets, orders, axis=1), jnp.take_along_axis(slots_all, orders, axis=1))


def draw_tile_slot(key, part):
    return tile_lists(key)[1]


def draw_tile_target(key, part):
    return tile_lists(key)[0]


def draw_send_counts(key, part):
    count_key, peak_key = jax.random.split(jax.random.fold_in(key, 5))
    counts = jax.random.randint(count_key, (PARTITIONS, N_BLK), 1, CAP + 1, dtype=jnp.int32)
    peak_reader = jax.random.randint(peak_key, (PARTITIONS, 1), 0, N_BLK, dtype=jnp.int32)
    readers = jnp.arange(N_BLK, dtype=jnp.int32)[None, :]
    return jnp.where(readers == peak_reader, CAP, counts).astype(jnp.int32)


def plant(drawn, key, low, largest):
    shape = drawn.shape
    spot = [jax.random.randint(jax.random.fold_in(key, axis), (), 0, shape[axis]) for axis in range(len(shape))]
    drawn = drawn.at[tuple(spot)].set(low)
    longest = shape.index(max(shape))
    spot[longest] = (spot[longest] + 1) % shape[longest]
    return drawn.at[tuple(spot)].set(largest)


def level_of(stream_key, extent, cuts, low, high):
    gain = 1.0
    for dim, parts in cuts:
        heights = jax.random.uniform(jax.random.fold_in(jax.random.fold_in(stream_key, 6), dim), (parts,), jnp.float32, low / len(cuts), high / len(cuts))
        gain = gain * jnp.repeat(jnp.exp(heights), extent[dim] // parts).reshape((-1,) + (1,) * (len(extent) - 1 - dim))
    return gain


def noise(stream_key, extent, spread, most, shards=(), kind=jnp.bfloat16):
    result = jax.random.normal(stream_key, extent, jnp.float32) * spread
    if len(shards) > 0:
        result = level_of(stream_key, extent, shards, -0.22, 0.18) * result
    return jnp.clip(result, min=-most, max=most).astype(kind)


def setup_inputs(seed: int = 0) -> dict:
    key_of = jax.random.split(jax.random.key(seed), 7)
    source = noise(key_of[0], (PARTITIONS * SB * BLOCK, COLS), 1.0, 6.0, ((0, 32),))
    send_ids = plant(jax.random.randint(key_of[1], (PARTITIONS, N_BLK * CAP), 0, SB), jax.random.fold_in(key_of[1], 1), 0, SB - 1).astype(jnp.int32)
    send_counts = draw_send_counts(jax.random.fold_in(key_of[6], 71), 0)
    tile_slot = draw_tile_slot(jax.random.fold_in(key_of[6], 71), 0)
    tile_target = draw_tile_target(jax.random.fold_in(key_of[6], 71), 0)
    tile_weights = jnp.clip(0.0625 * jax.random.uniform(key_of[5], (PARTITIONS * NT, BLOCK * BLOCK), jnp.float32) ** level_of(key_of[5], (PARTITIONS * NT, BLOCK * BLOCK), ((0, 32),), -0.2, 0.2), 0.0, 0.0625).astype(jnp.bfloat16)
    return dict(source=source, send_ids=send_ids, send_counts=send_counts, tile_slot=tile_slot, tile_target=tile_target, tile_weights=tile_weights)


def device_partial(device, source, send_ids, send_counts, tile_slot, tile_target, tile_weights):
    group_index = device // N_BLK
    reader_index = device % N_BLK
    senders = group_index * N_BLK + jnp.arange(N_BLK, dtype=jnp.int32)
    sender_ids = jnp.take(send_ids, senders, axis=0)
    block_ids = lax.dynamic_slice_in_dim(sender_ids, reader_index * CAP, CAP, 1)
    sender_counts = jnp.take(send_counts, senders, axis=0)
    live_counts = lax.dynamic_slice_in_dim(sender_counts, reader_index, 1, 1)[:, 0]
    source_blocks = source.reshape(PARTITIONS, SB, BLOCK, COLS)
    chosen = source_blocks[senders[:, None], block_ids]
    live_mask = jnp.arange(CAP, dtype=jnp.int32)[None, :] < live_counts[:, None]
    chosen = jnp.where(live_mask[:, :, None, None], chosen, jnp.zeros_like(chosen))
    received = chosen.reshape(N_BLK * CAP, BLOCK, COLS)
    tile_slots = lax.dynamic_index_in_dim(tile_slot, device, 0, keepdims=False)
    tile_targets = lax.dynamic_index_in_dim(tile_target, device, 0, keepdims=False)
    operands = jnp.take(received, tile_slots, axis=0).astype(jnp.float32)
    weights = lax.dynamic_slice_in_dim(tile_weights, device * NT, NT, 0)
    weights = weights.reshape(NT, BLOCK, BLOCK).astype(jnp.float32)
    products = jnp.einsum("kij,kjc->kic", weights, operands, precision=lax.Precision.HIGHEST)
    return jax.ops.segment_sum(products, tile_targets, num_segments=TB + 2 * EB)


def reference(source, send_ids, send_counts, tile_slot, tile_target, tile_weights):
    compute = partial(device_partial, source=source, send_ids=send_ids, send_counts=send_counts,
                      tile_slot=tile_slot, tile_target=tile_target, tile_weights=tile_weights)
    first_pieces = compute(jnp.int32(0))
    final_pieces = compute(jnp.int32(PARTITIONS - 1))

    def advance(running, device):
        prior_own, prior_upper = running
        pieces = compute(device)
        lower_edge = pieces[:EB]
        middle = pieces[EB:EB + TB]
        upper_edge = pieces[EB + TB:]
        finished = jnp.concatenate([prior_own[:TB - EB], prior_own[TB - EB:] + lower_edge], axis=0)
        current = jnp.concatenate([middle[:EB] + prior_upper, middle[EB:]], axis=0)
        return (current, upper_edge), finished

    start_running = (jnp.zeros((TB, BLOCK, COLS), jnp.float32), final_pieces[EB + TB:])
    devices = jnp.arange(PARTITIONS, dtype=jnp.int32)
    (last_own, last_upper), emitted = lax.scan(advance, start_running, devices)
    last_done = jnp.concatenate([last_own[:TB - EB], last_own[TB - EB:] + first_pieces[:EB]], axis=0)
    assembled = jnp.concatenate([emitted[1:], last_done[None]], axis=0)
    return assembled.reshape(PARTITIONS * TB * BLOCK, COLS)
```

```python
import functools

import jax
import jax.numpy as jnp
from jax import lax
from jax.experimental import pallas as pl
from jax.experimental.pallas import tpu as pltpu
from jax.sharding import PartitionSpec as P

COLS = 256
BLOCK = 64
EB = 16
CHUNK = 2 * BLOCK
ROWS = EB * BLOCK
GROUP = 64
GROUPS = ROWS // GROUP
FLOOR = 2.0**-110
VMEM = pl.BlockSpec(memory_space=pltpu.VMEM)
SMEM = pl.BlockSpec(memory_space=pltpu.SMEM)
ANY = pl.BlockSpec(memory_space=pl.ANY)


def params():
    return pltpu.CompilerParams(vmem_limit_bytes=40 * 1024 * 1024)


def cost(flops, nbytes):
    return pl.CostEstimate(flops=flops, bytes_accessed=nbytes, transcendentals=0)


def pick_kernel(members, capacity, ids, counts, source, *refs):
    outs, sems = refs[:members], refs[members]
    own = lax.axis_index("blk")
    copies = []
    for k in range(members):
        reader = lax.rem(own + k, members)
        for j in range(capacity):
            start = pl.multiple_of(ids[0, reader * capacity + j] * BLOCK, BLOCK)
            copy = pltpu.make_async_copy(
                source.at[pl.ds(start, BLOCK)],
                outs[k].at[pl.ds(j * BLOCK, BLOCK)],
                sems.at[k * capacity + j],
            )
            copy.start()
            copies.append(copy)
    for copy in copies:
        copy.wait()
    for k in range(members):
        reader = lax.rem(own + k, members)
        for j in range(capacity):

            @pl.when(j >= counts[0, reader])
            def _():
                outs[k][pl.ds(j * BLOCK, BLOCK)] = jnp.zeros((BLOCK, COLS), jnp.bfloat16)


def pick(members, capacity, send_ids, send_counts, source):
    shape = (capacity * BLOCK, COLS)
    return pl.pallas_call(
        functools.partial(pick_kernel, members, capacity),
        out_shape=[pltpu.VMEM(shape, jnp.bfloat16)] * members,
        in_specs=[SMEM, SMEM, ANY],
        out_specs=[VMEM] * members,
        scratch_shapes=[pltpu.SemaphoreType.DMA((members * capacity,))],
        compiler_params=params(),
        name="pick",
    )(send_ids, send_counts, source)


def spread_kernel(members, capacity, quarters, slots, targets, weights, *outs):
    own = lax.axis_index("blk")
    tiles = weights.shape[0]
    width = members * CHUNK
    count = len(quarters)
    slot = slots[...]
    sender = slot // capacity
    shift = lax.rem(own - sender + members, members)
    place = shift * capacity + slot % capacity
    target = targets[...]
    rows = lax.broadcasted_iota(jnp.int32, (count * EB, tiles), 0)
    wanted = rows
    for n, q in enumerate(quarters):
        wanted = jnp.where(rows // EB == n, rows % EB + q * EB, wanted)
    hit = target == wanted
    table = jnp.concatenate(
        [
            jnp.concatenate(
                [(hit & (place == k * capacity + j)).astype(jnp.float32) for j in range(capacity)], axis=1
            )
            for k in range(members)
        ],
        axis=0,
    ).astype(jnp.bfloat16)
    left = (lax.broadcasted_iota(jnp.int32, (1, CHUNK), 1) < BLOCK).astype(jnp.float32)
    low = left.astype(jnp.bfloat16)
    high = (1.0 - left).astype(jnp.bfloat16)

    def step(c, _):
        x = weights[:, pl.ds(pl.multiple_of(c * CHUNK, CHUNK), CHUNK)]
        swapped = jnp.concatenate([x[:, BLOCK:], x[:, :BLOCK]], axis=1)
        right = jnp.concatenate(
            [
                jnp.concatenate([x * low, swapped * low], axis=1),
                jnp.concatenate([swapped * high, x * high], axis=1),
            ],
            axis=0,
        )
        sums = jnp.dot(table, right, preferred_element_type=jnp.float32)
        coarse = sums.astype(jnp.bfloat16)
        fine = (sums - coarse.astype(jnp.float32)).astype(jnp.bfloat16)
        for k in range(members):
            for n in range(count):
                top = (k * count + n) * EB
                for h in range(2):
                    row = pl.ds(pl.multiple_of((2 * c + h) * EB, EB), EB)
                    part = (slice(top, top + EB), slice(h * CHUNK, (h + 1) * CHUNK))
                    outs[n][row, k * CHUNK : (k + 1) * CHUNK] = coarse[part]
                    outs[n][row, width + k * CHUNK : width + (k + 1) * CHUNK] = fine[part]
        return 0

    lax.fori_loop(0, BLOCK // 2, step, 0, unroll=2)


def spread(members, capacity, quarters, slots, targets, weights):
    shape = (ROWS, 2 * members * CHUNK)
    tiles = weights.shape[0]
    return pl.pallas_call(
        functools.partial(spread_kernel, members, capacity, quarters),
        out_shape=[pltpu.VMEM(shape, jnp.bfloat16)] * len(quarters),
        in_specs=[VMEM] * 3,
        out_specs=[VMEM] * len(quarters),
        compiler_params=params(),
        cost_estimate=cost(2 * members * EB * len(quarters) * 2 * tiles * 8192, 6 * 2**20),
        name="spread",
    )(slots, targets, weights)


def stack(blocks, both):
    rows = blocks[0].shape[0]
    for half in range(2):
        for k, block in enumerate(blocks):
            start = (half * len(blocks) + k) * rows
            both[start : start + rows] = block[...]


def edge_kernel(members, left, *refs):
    blocks, message, both, powers = refs[:members], refs[members], refs[members + 1], refs[members + 2]
    stack(blocks, both)
    step = 4 * GROUP
    for start in range(0, ROWS, step):
        piece = jnp.dot(left[start : start + step], both[...], preferred_element_type=jnp.float32)
        for g in range(step // GROUP):
            rows = piece[g * GROUP : (g + 1) * GROUP]
            most = jnp.maximum(jnp.max(jnp.abs(rows), axis=0, keepdims=True), FLOOR)
            power = jnp.floor(jnp.log2(most) + 0.001) + 1.0
            whole = jnp.round(rows * jnp.exp2(15.0 - power)).astype(jnp.int32)
            message[start + g * GROUP : start + (g + 1) * GROUP] = whole.astype(jnp.int16)
            at = start // GROUP + g
            powers[at : at + 1] = power.astype(jnp.int32)
    message[ROWS : ROWS + GROUPS] = powers[...].astype(jnp.int16)


def edge(members, left, blocks):
    return pl.pallas_call(
        functools.partial(edge_kernel, members),
        out_shape=pltpu.VMEM((ROWS + GROUPS, COLS), jnp.int16),
        in_specs=[VMEM] * (1 + members),
        out_specs=VMEM,
        scratch_shapes=[
            pltpu.VMEM((left.shape[1], COLS), jnp.bfloat16),
            pltpu.VMEM((GROUPS, COLS), jnp.int32),
        ],
        compiler_params=params(),
        cost_estimate=cost(2 * ROWS * left.shape[1] * COLS, 2 * 2**20),
        name="edge",
    )(left, *blocks)


def middle_kernel(members, first, second, *refs):
    blocks, outs, both = refs[:members], refs[members : members + 2], refs[members + 2]
    stack(blocks, both)
    step = 256
    for left, out in zip((first, second), outs):
        for start in range(0, ROWS, step):
            out[start : start + step] = jnp.dot(
                left[start : start + step], both[...], preferred_element_type=jnp.float32
            )


def middle(members, first, second, blocks):
    return pl.pallas_call(
        functools.partial(middle_kernel, members),
        out_shape=[pltpu.VMEM((ROWS, COLS), jnp.float32)] * 2,
        in_specs=[VMEM] * (2 + members),
        out_specs=[VMEM] * 2,
        scratch_shapes=[pltpu.VMEM((first.shape[1], COLS), jnp.bfloat16)],
        compiler_params=params(),
        cost_estimate=cost(4 * ROWS * first.shape[1] * COLS, 4 * 2**20),
        name="middle",
    )(first, second, *blocks)


def finish_kernel(half, own, message, *refs):
    out, rows, sems = refs[-3:]
    scale = jnp.exp2(message[ROWS : ROWS + GROUPS].astype(jnp.float32) - 15.0)
    for i in range(BLOCK):
        at = i * EB
        g = at // GROUP
        value = own[at : at + EB] + message[at : at + EB].astype(jnp.float32) * scale[g : g + 1]
        for n in range(COLS // 128):
            rows[n, pl.ds(i, EB, stride=BLOCK)] = value[:, n * 128 : (n + 1) * 128]
    copies = []
    for n in range(COLS // 128):
        there = out.at[pl.ds(half * ROWS, ROWS), pl.ds(n * 128, 128)]
        copies.append(pltpu.make_async_copy(rows.at[n], there, sems.at[n]))
        copies[n].start()
    for copy in copies:
        copy.wait()


def finish(half, own, message, out=None):
    given = [] if out is None else [out]
    return pl.pallas_call(
        functools.partial(finish_kernel, half),
        out_shape=jax.ShapeDtypeStruct((2 * ROWS, COLS), jnp.float32),
        in_specs=[VMEM] * 2 + [ANY] * len(given),
        out_specs=ANY,
        scratch_shapes=[
            pltpu.VMEM((COLS // 128, ROWS, 128), jnp.float32),
            pltpu.SemaphoreType.DMA((COLS // 128,)),
        ],
        input_output_aliases={} if out is None else {2: 0},
        compiler_params=params(),
        cost_estimate=cost(3 * ROWS * COLS, 2 * 2**20),
        name="finish",
    )(own, message, *given)


def passed_along(shard, axis, by):
    count = lax.axis_size(axis)
    return lax.ppermute(shard, axis, [(i, (i + by) % count) for i in range(count)])


def body(source, send_ids, send_counts, tile_slot, tile_target, tile_weights):
    members = lax.axis_size("blk")
    capacity = send_ids.shape[1] // members
    picked = pick(members, capacity, send_ids, send_counts, source)
    blocks = [picked[0]] + [passed_along(picked[k], "blk", k) for k in range(1, members)]
    tiles = (tile_slot, tile_target, tile_weights)
    lower, upper = spread(members, capacity, (0, 3), *tiles)
    first, second = spread(members, capacity, (1, 2), *tiles)
    from_prior = passed_along(edge(members, upper, blocks), ("grp", "blk"), 1)
    from_next = passed_along(edge(members, lower, blocks), ("grp", "blk"), -1)
    own_first, own_second = middle(members, first, second, blocks)
    out = finish(0, own_first, from_prior)
    return finish(1, own_second, from_next, out)


def solution(mesh):
    spec = P(("grp", "blk"), None)
    return jax.shard_map(body, mesh=mesh, in_specs=(spec,) * 6, out_specs=spec, check_vma=False)
```

```python
import functools

import jax
import jax.numpy as jnp
from jax import lax
from jax.experimental import pallas as pl
from jax.experimental.pallas import tpu as pltpu
from jax.sharding import PartitionSpec as P

COLS = 256
BLOCK = 64
EB = 16
CHUNK = 2 * BLOCK
ROWS = EB * BLOCK
GROUP = 64
GROUPS = ROWS // GROUP
FLOOR = 2.0**-110
PITCH = BLOCK + 8
VMEM = pl.BlockSpec(memory_space=pltpu.VMEM)
SMEM = pl.BlockSpec(memory_space=pltpu.SMEM)
ANY = pl.BlockSpec(memory_space=pl.ANY)


def params():
    return pltpu.CompilerParams(vmem_limit_bytes=40 * 1024 * 1024)


def cost(flops, nbytes):
    return pl.CostEstimate(flops=flops, bytes_accessed=nbytes, transcendentals=0)


def partner(own, k, members):
    if members & (members - 1) == 0:
        return lax.bitwise_xor(own, jnp.int32(k))
    return lax.rem(own + k, members)


def step_of(own, sender, members):
    if members & (members - 1) == 0:
        return lax.bitwise_xor(jnp.full_like(sender, own), sender)
    return lax.rem(own - sender + members, members)


def pick_kernel(members, capacity, ids, counts, source, *refs):
    fed, refs = refs[:3], refs[3:]
    picked, held, refs = refs[:members], refs[members : members + 3], refs[members + 3 :]
    blocks, id_list, count_list, sems = refs
    own = lax.axis_index("blk")
    copies = [
        pltpu.make_async_copy(here, there, sems.at[n])
        for n, (here, there) in enumerate(
            zip((ids, counts, source) + fed, (id_list, count_list, blocks) + held)
        )
    ]
    for copy in copies:
        copy.start()
    for copy in copies[:3]:
        copy.wait()
    for k in range(members):
        reader = partner(own, k, members)
        for j in range(capacity):
            start = pl.multiple_of(id_list[0, reader * capacity + j] * BLOCK, BLOCK)
            live = (j < count_list[0, reader]).astype(jnp.float32).astype(jnp.bfloat16)
            picked[k][j * BLOCK : (j + 1) * BLOCK] = blocks[pl.ds(start, BLOCK)] * live
    for copy in copies[3:]:
        copy.wait()


def pick(members, capacity, send_ids, send_counts, source, *fed):
    shape = (capacity * BLOCK, COLS)
    given = [pltpu.with_memory_space_constraint(x, pltpu.HBM) for x in (send_ids, send_counts, source) + fed]
    results = pl.pallas_call(
        functools.partial(pick_kernel, members, capacity),
        out_shape=[pltpu.VMEM(shape, jnp.bfloat16)] * members + [pltpu.VMEM(x.shape, x.dtype) for x in fed],
        in_specs=[ANY] * len(given),
        out_specs=[VMEM] * (members + len(fed)),
        scratch_shapes=[
            pltpu.VMEM(source.shape, source.dtype),
            pltpu.SMEM(send_ids.shape, jnp.int32),
            pltpu.SMEM(send_counts.shape, jnp.int32),
            pltpu.SemaphoreType.DMA((len(given),)),
        ],
        compiler_params=params(),
        name="pick",
    )(*given)
    return results[:members], results[members:]


def spread_kernel(members, capacity, quarters, slots, targets, weights, *outs):
    own = lax.axis_index("blk")
    tiles = weights.shape[0]
    width = members * CHUNK
    count = len(quarters)
    slot = slots[...]
    sender = slot // capacity
    place = step_of(own, sender, members) * capacity + slot % capacity
    target = targets[...]
    rows = lax.broadcasted_iota(jnp.int32, (count * EB, tiles), 0)
    wanted = rows
    for n, q in enumerate(quarters):
        wanted = jnp.where(rows // EB == n, rows % EB + q * EB, wanted)
    hit = target == wanted
    table = jnp.concatenate(
        [
            jnp.concatenate(
                [(hit & (place == k * capacity + j)).astype(jnp.float32) for j in range(capacity)], axis=1
            )
            for k in range(members)
        ],
        axis=0,
    ).astype(jnp.bfloat16)
    left = (lax.broadcasted_iota(jnp.int32, (1, CHUNK), 1) < BLOCK).astype(jnp.float32)
    low = left.astype(jnp.bfloat16)
    high = (1.0 - left).astype(jnp.bfloat16)

    def step(c, _):
        x = weights[:, pl.ds(pl.multiple_of(c * CHUNK, CHUNK), CHUNK)]
        swapped = jnp.concatenate([x[:, BLOCK:], x[:, :BLOCK]], axis=1)
        right = jnp.concatenate(
            [
                jnp.concatenate([x * low, swapped * low], axis=1),
                jnp.concatenate([swapped * high, x * high], axis=1),
            ],
            axis=0,
        )
        sums = jnp.dot(table, right, preferred_element_type=jnp.float32)
        coarse = sums.astype(jnp.bfloat16)
        fine = (sums - coarse.astype(jnp.float32)).astype(jnp.bfloat16)
        for k in range(members):
            for n in range(count):
                top = (k * count + n) * EB
                for h in range(2):
                    row = pl.ds(pl.multiple_of((2 * c + h) * EB, EB), EB)
                    part = (slice(top, top + EB), slice(h * CHUNK, (h + 1) * CHUNK))
                    outs[n][row, k * CHUNK : (k + 1) * CHUNK] = coarse[part]
                    outs[n][row, width + k * CHUNK : width + (k + 1) * CHUNK] = fine[part]
        return 0

    lax.fori_loop(0, BLOCK // 2, step, 0, unroll=8)


def spread(members, capacity, quarters, slots, targets, weights):
    shape = (ROWS, 2 * members * CHUNK)
    tiles = weights.shape[0]
    return pl.pallas_call(
        functools.partial(spread_kernel, members, capacity, quarters),
        out_shape=[pltpu.VMEM(shape, jnp.bfloat16)] * len(quarters),
        in_specs=[VMEM] * 3,
        out_specs=[VMEM] * len(quarters),
        compiler_params=params(),
        cost_estimate=cost(2 * members * EB * len(quarters) * 2 * tiles * 8192, 6 * 2**20),
        name="spread",
    )(slots, targets, weights)


def stack(blocks, both):
    rows = blocks[0].shape[0]
    for half in range(2):
        for k, block in enumerate(blocks):
            start = (half * len(blocks) + k) * rows
            both[start : start + rows] = block[...]


def edge_kernel(members, left, *refs):
    blocks, message, both, powers = refs[:members], refs[members], refs[members + 1], refs[members + 2]
    stack(blocks, both)
    step = 4 * GROUP
    for start in range(0, ROWS, step):
        piece = jnp.dot(left[start : start + step], both[...], preferred_element_type=jnp.float32)
        for g in range(step // GROUP):
            rows = piece[g * GROUP : (g + 1) * GROUP]
            most = jnp.maximum(jnp.max(jnp.abs(rows), axis=0, keepdims=True), FLOOR)
            power = jnp.floor(jnp.log2(most) + 0.001) + 1.0
            whole = jnp.round(rows * jnp.exp2(15.0 - power)).astype(jnp.int32)
            message[start + g * GROUP : start + (g + 1) * GROUP] = whole.astype(jnp.int16)
            at = start // GROUP + g
            powers[at : at + 1] = power.astype(jnp.int32)
    message[ROWS : ROWS + GROUPS] = powers[...].astype(jnp.int16)


def edge(members, left, blocks):
    return pl.pallas_call(
        functools.partial(edge_kernel, members),
        out_shape=pltpu.VMEM((ROWS + GROUPS, COLS), jnp.int16),
        in_specs=[VMEM] * (1 + members),
        out_specs=VMEM,
        scratch_shapes=[
            pltpu.VMEM((left.shape[1], COLS), jnp.bfloat16),
            pltpu.VMEM((GROUPS, COLS), jnp.int32),
        ],
        compiler_params=params(),
        cost_estimate=cost(2 * ROWS * left.shape[1] * COLS, 2 * 2**20),
        name="edge",
    )(left, *blocks)


def middle_kernel(members, first, second, *refs):
    blocks, outs, both = refs[:members], refs[members : members + 2], refs[members + 2]
    stack(blocks, both)
    step = 256
    for left, out in zip((first, second), outs):
        for start in range(0, ROWS, step):
            out[start : start + step] = jnp.dot(
                left[start : start + step], both[...], preferred_element_type=jnp.float32
            )


def middle(members, first, second, blocks):
    return pl.pallas_call(
        functools.partial(middle_kernel, members),
        out_shape=[pltpu.VMEM((ROWS, COLS), jnp.float32)] * 2,
        in_specs=[VMEM] * (2 + members),
        out_specs=[VMEM] * 2,
        scratch_shapes=[pltpu.VMEM((first.shape[1], COLS), jnp.bfloat16)],
        compiler_params=params(),
        cost_estimate=cost(4 * ROWS * first.shape[1] * COLS, 4 * 2**20),
        name="middle",
    )(first, second, *blocks)


def finish_kernel(half, own, message, *refs):
    out, rows, sems = refs[-3:]
    scale = jnp.exp2(message[ROWS : ROWS + GROUPS].astype(jnp.float32) - 15.0)
    targets = rows.reshape(COLS // 128, EB, PITCH, 128)
    some = EB // 2
    copies = []
    for first in range(0, EB, some):
        for i in range(BLOCK):
            at = i * EB
            g = at // GROUP
            value = message[at : at + EB].astype(jnp.float32)[first : first + some]
            value = own[at + first : at + first + some] + value * scale[g : g + 1]
            for n in range(COLS // 128):
                place = pl.ds(first * PITCH + i, some, stride=PITCH)
                rows[n, place] = value[:, n * 128 : (n + 1) * 128]
        for n in range(COLS // 128):
            here = targets.at[n, pl.ds(first, some), pl.ds(0, BLOCK)]
            there = out.at[pl.ds(half * EB + first, some), :, pl.ds(n * 128, 128)]
            copies.append(pltpu.make_async_copy(here, there, sems.at[len(copies)]))
            copies[-1].start()
    for copy in copies:
        copy.wait()


def finish(half, own, message, out=None):
    given = [] if out is None else [out]
    return pl.pallas_call(
        functools.partial(finish_kernel, half),
        out_shape=jax.ShapeDtypeStruct((2 * EB, BLOCK, COLS), jnp.float32),
        in_specs=[VMEM] * 2 + [ANY] * len(given),
        out_specs=ANY,
        scratch_shapes=[
            pltpu.VMEM((COLS // 128, EB * PITCH, 128), jnp.float32),
            pltpu.SemaphoreType.DMA((2 * COLS // 128,)),
        ],
        input_output_aliases={} if out is None else {2: 0},
        compiler_params=params(),
        cost_estimate=cost(3 * ROWS * COLS, 2 * 2**20),
        name="finish",
    )(own, message, *given)


def passed_along(shard, axis, by):
    count = lax.axis_size(axis)
    return lax.ppermute(shard, axis, [(i, (i + by) % count) for i in range(count)])


def exchanged(shard, k):
    members = lax.axis_size("blk")
    if members & (members - 1) == 0:
        return lax.ppermute(shard, "blk", [(i, i ^ k) for i in range(members)])
    return passed_along(shard, "blk", k)


def body(source, send_ids, send_counts, tile_slot, tile_target, tile_weights):
    members = lax.axis_size("blk")
    capacity = send_ids.shape[1] // members
    picked, tiles = pick(
        members, capacity, send_ids, send_counts, source, tile_slot, tile_target, tile_weights
    )
    blocks = [picked[0]] + [exchanged(picked[k], k) for k in range(1, members)]
    lower, upper = spread(members, capacity, (0, 3), *tiles)
    first, second = spread(members, capacity, (1, 2), *tiles)
    from_prior = passed_along(edge(members, upper, blocks), ("grp", "blk"), 1)
    from_next = passed_along(edge(members, lower, blocks), ("grp", "blk"), -1)
    own_first, own_second = middle(members, first, second, blocks)
    out = finish(0, own_first, from_prior)
    out = finish(1, own_second, from_next, out)
    return out.reshape(2 * ROWS, COLS)


def solution(mesh):
    spec = P(("grp", "blk"), None)
    return jax.shard_map(body, mesh=mesh, in_specs=(spec,) * 6, out_specs=spec, check_vma=False)
```

```python
import functools

import jax
import jax.numpy as jnp
from jax import lax
from jax.experimental import pallas as pl
from jax.experimental.pallas import tpu as pltpu
from jax.sharding import PartitionSpec as P

COLS = 256
BLOCK = 64
EB = 16
CHUNK = 2 * BLOCK
ROWS = EB * BLOCK
GROUP = 32
FLOOR = 2.0**-110
VMEM = pl.BlockSpec(memory_space=pltpu.VMEM)
SMEM = pl.BlockSpec(memory_space=pltpu.SMEM)
ANY = pl.BlockSpec(memory_space=pl.ANY)


def params():
    return pltpu.CompilerParams(vmem_limit_bytes=40 * 1024 * 1024)


def cost(flops, nbytes):
    return pl.CostEstimate(flops=flops, bytes_accessed=nbytes, transcendentals=0)


def parity():
    return lax.rem(lax.axis_index("grp") * lax.axis_size("blk") + lax.axis_index("blk"), 2)


def partner(own, k, members):
    if members & (members - 1) == 0:
        return lax.bitwise_xor(own, jnp.int32(k))
    return lax.rem(own + k, members)


def step_of(own, sender, members):
    if members & (members - 1) == 0:
        return lax.bitwise_xor(jnp.full_like(sender, own), sender)
    return lax.rem(own - sender + members, members)


def pick_kernel(members, capacity, ids, counts, source, *refs):
    fed, refs = refs[:3], refs[3:]
    picked, held, refs = refs[:members], refs[members : members + 3], refs[members + 3 :]
    blocks, id_list, count_list, sems = refs
    own = lax.axis_index("blk")
    copies = [
        pltpu.make_async_copy(here, there, sems.at[n])
        for n, (here, there) in enumerate(
            zip((ids, counts, source) + fed, (id_list, count_list, blocks) + held)
        )
    ]
    for copy in copies:
        copy.start()
    for copy in copies[:3]:
        copy.wait()
    for k in range(members):
        reader = partner(own, k, members)
        for j in range(capacity):
            start = pl.multiple_of(id_list[0, reader * capacity + j] * BLOCK, BLOCK)
            live = (j < count_list[0, reader]).astype(jnp.float32).astype(jnp.bfloat16)
            picked[k][j * BLOCK : (j + 1) * BLOCK] = blocks[pl.ds(start, BLOCK)] * live
    for copy in copies[3:]:
        copy.wait()


def pick(members, capacity, send_ids, send_counts, source, *fed):
    shape = (capacity * BLOCK, COLS)
    given = [pltpu.with_memory_space_constraint(x, pltpu.HBM) for x in (send_ids, send_counts, source) + fed]
    results = pl.pallas_call(
        functools.partial(pick_kernel, members, capacity),
        out_shape=[pltpu.VMEM(shape, jnp.bfloat16)] * members + [pltpu.VMEM(x.shape, x.dtype) for x in fed],
        in_specs=[ANY] * len(given),
        out_specs=[VMEM] * (members + len(fed)),
        scratch_shapes=[
            pltpu.VMEM(source.shape, source.dtype),
            pltpu.SMEM(send_ids.shape, jnp.int32),
            pltpu.SMEM(send_counts.shape, jnp.int32),
            pltpu.SemaphoreType.DMA((len(given),)),
        ],
        compiler_params=params(),
        name="pick",
    )(*given)
    return results[:members], results[members:]


def spread_kernel(members, capacity, quarters, slots, targets, weights, *outs):
    own = lax.axis_index("blk")
    tiles = weights.shape[0]
    width = members * CHUNK
    count = len(quarters)
    slot = slots[...]
    sender = slot // capacity
    place = step_of(own, sender, members) * capacity + slot % capacity
    target = targets[...]
    rows = lax.broadcasted_iota(jnp.int32, (count * EB, tiles), 0)
    wanted = rows
    for n, (even, odd) in enumerate(quarters):
        wanted = jnp.where(rows // EB == n, rows % EB + jnp.where(parity() == 1, odd, even) * EB, wanted)
    hit = target == wanted
    table = jnp.concatenate(
        [
            jnp.concatenate(
                [(hit & (place == k * capacity + j)).astype(jnp.float32) for j in range(capacity)], axis=1
            )
            for k in range(members)
        ],
        axis=0,
    ).astype(jnp.bfloat16)
    left = (lax.broadcasted_iota(jnp.int32, (1, CHUNK), 1) < BLOCK).astype(jnp.float32)
    low = left.astype(jnp.bfloat16)
    high = (1.0 - left).astype(jnp.bfloat16)

    def step(c, _):
        x = weights[:, pl.ds(pl.multiple_of(c * CHUNK, CHUNK), CHUNK)]
        swapped = jnp.concatenate([x[:, BLOCK:], x[:, :BLOCK]], axis=1)
        right = jnp.concatenate(
            [
                jnp.concatenate([x * low, swapped * low], axis=1),
                jnp.concatenate([swapped * high, x * high], axis=1),
            ],
            axis=0,
        )
        sums = jnp.dot(table, right, preferred_element_type=jnp.float32)
        coarse = sums.astype(jnp.bfloat16)
        fine = (sums - coarse.astype(jnp.float32)).astype(jnp.bfloat16)
        for k in range(members):
            for n in range(count):
                top = (k * count + n) * EB
                for h in range(2):
                    row = pl.ds(pl.multiple_of((2 * c + h) * EB, EB), EB)
                    part = (slice(top, top + EB), slice(h * CHUNK, (h + 1) * CHUNK))
                    outs[n][row, k * CHUNK : (k + 1) * CHUNK] = coarse[part]
                    outs[n][row, width + k * CHUNK : width + (k + 1) * CHUNK] = fine[part]
        return 0

    lax.fori_loop(0, BLOCK // 2, step, 0, unroll=8)


def spread(members, capacity, quarters, slots, targets, weights):
    shape = (ROWS, 2 * members * CHUNK)
    tiles = weights.shape[0]
    return pl.pallas_call(
        functools.partial(spread_kernel, members, capacity, quarters),
        out_shape=[pltpu.VMEM(shape, jnp.bfloat16)] * len(quarters),
        in_specs=[VMEM] * 3,
        out_specs=[VMEM] * len(quarters),
        compiler_params=params(),
        cost_estimate=cost(2 * members * EB * len(quarters) * 2 * tiles * 8192, 6 * 2**20),
        name="spread",
    )(slots, targets, weights)


def stack_kernel(blocks, both):
    rows = blocks[0].shape[0]
    for half in range(2):
        for k, block in enumerate(blocks):
            start = (half * len(blocks) + k) * rows
            both[start : start + rows] = block[...]


def edge_kernel(first, count, blocks, left, *refs):
    if blocks:
        received, (message, both, powers) = refs[:blocks], refs[blocks:]
        stack_kernel(received, both)
    else:
        both, message, powers = refs
    step = min(count, 256)
    for start in range(0, count, step):
        rows = left[first + start : first + start + step]
        piece = jnp.dot(rows, both[...], preferred_element_type=jnp.float32)
        for g in range(step // GROUP):
            rows = piece[g * GROUP : (g + 1) * GROUP]
            most = jnp.maximum(jnp.max(jnp.abs(rows), axis=0, keepdims=True), FLOOR)
            power = jnp.floor(jnp.log2(most) + 0.001) + 1.0
            whole = jnp.round(rows * jnp.exp2(15.0 - power)).astype(jnp.int32)
            message[start + g * GROUP : start + (g + 1) * GROUP] = whole.astype(jnp.int16)
            at = start // GROUP + g
            powers[at : at + 1] = power.astype(jnp.int32)
    message[count : count + count // GROUP] = powers[...].astype(jnp.int16)


def edge(first, count, left, *right):
    out_shape = [pltpu.VMEM((count + count // GROUP, COLS), jnp.int16)]
    if len(right) > 1:
        out_shape.append(pltpu.VMEM((left.shape[1], COLS), jnp.bfloat16))
    return pl.pallas_call(
        functools.partial(edge_kernel, first, count, len(right) if len(right) > 1 else 0),
        out_shape=out_shape,
        in_specs=[VMEM] * (1 + len(right)),
        out_specs=[VMEM] * len(out_shape),
        scratch_shapes=[pltpu.VMEM((count // GROUP, COLS), jnp.int32)],
        compiler_params=params(),
        cost_estimate=cost(2 * count * left.shape[1] * COLS, 2 * 2**20),
        name="edge",
    )(left, *right)


def middle_kernel(first, second, both, *outs):
    step = 256
    for left, out in zip((first, second), outs):
        for start in range(0, ROWS, step):
            out[start : start + step] = jnp.dot(
                left[start : start + step], both[...], preferred_element_type=jnp.float32
            )


def middle(first, second, both):
    return pl.pallas_call(
        middle_kernel,
        out_shape=[pltpu.VMEM((ROWS, COLS), jnp.float32)] * 2,
        in_specs=[VMEM] * 3,
        out_specs=[VMEM] * 2,
        compiler_params=params(),
        cost_estimate=cost(4 * ROWS * first.shape[1] * COLS, 4 * 2**20),
        name="middle",
    )(first, second, both)


def finish_kernel(across, low, high, own, message, *refs):
    out, rows, sems = refs[-3:]
    half = parity() if across else 1 - parity()
    count = (high - low) * EB
    pitch = high - low + 8
    scale = jnp.exp2(message[count : count + count // GROUP].astype(jnp.float32) - 15.0)
    targets = rows.reshape(COLS // 128, EB, pitch, 128)
    some = EB // 2
    copies = []
    for first in range(0, EB, some):
        for i in range(high - low):
            at = i * EB
            g = at // GROUP
            value = message[at : at + EB].astype(jnp.float32)[first : first + some]
            at = (low + i) * EB + first
            value = own[at : at + some] + value * scale[g : g + 1]
            for n in range(COLS // 128):
                place = pl.ds(first * pitch + i, some, stride=pitch)
                rows[n, place] = value[:, n * 128 : (n + 1) * 128]
        for n in range(COLS // 128):
            here = targets.at[n, pl.ds(first, some), pl.ds(0, high - low)]
            there = out.at[pl.ds(half * EB + first, some), pl.ds(low, high - low), pl.ds(n * 128, 128)]
            copies.append(pltpu.make_async_copy(here, there, sems.at[len(copies)]))
            copies[-1].start()
    for copy in copies:
        copy.wait()


def finish(across, low, high, own, message, out=None):
    given = [] if out is None else [out]
    return pl.pallas_call(
        functools.partial(finish_kernel, across, low, high),
        out_shape=jax.ShapeDtypeStruct((2 * EB, BLOCK, COLS), jnp.float32),
        in_specs=[VMEM] * 2 + [ANY] * len(given),
        out_specs=ANY,
        scratch_shapes=[
            pltpu.VMEM((COLS // 128, EB * (high - low + 8), 128), jnp.float32),
            pltpu.SemaphoreType.DMA((2 * COLS // 128,)),
        ],
        input_output_aliases={} if out is None else {2: 0},
        compiler_params=params(),
        cost_estimate=cost(3 * (high - low) * EB * COLS, 2 * 2**20),
        name="finish",
    )(own, message, *given)


def passed_along(shard, axis, by):
    count = lax.axis_size(axis)
    return lax.ppermute(shard, axis, [(i, (i + by) % count) for i in range(count)])


def exchanged(shard, k):
    members = lax.axis_size("blk")
    if members & (members - 1) == 0:
        return lax.ppermute(shard, "blk", [(i, i ^ k) for i in range(members)])
    return passed_along(shard, "blk", k)


def ring_swap(shard, across):
    axes = ("grp", "blk")
    count = lax.axis_size(axes)
    if across:
        return lax.ppermute(shard, axes, [(i, (i + (1 if i % 2 else -1)) % count) for i in range(count)])
    return lax.ppermute(shard, axes, [(i, i ^ 1) for i in range(count)])


def body(source, send_ids, send_counts, tile_slot, tile_target, tile_weights):
    members = lax.axis_size("blk")
    capacity = send_ids.shape[1] // members
    picked, tiles = pick(
        members, capacity, send_ids, send_counts, source, tile_slot, tile_target, tile_weights
    )
    blocks = [picked[0]] + [exchanged(picked[k], k) for k in range(1, members)]
    left_across, left_chip = spread(members, capacity, ((0, 3), (3, 0)), *tiles)
    own_left = spread(members, capacity, ((1, 2), (2, 1)), *tiles)
    half = ROWS // 2
    message_0, both = edge(0, half, left_across, *blocks)
    message_0 = ring_swap(message_0, True)
    message_1 = ring_swap(edge(half, half, left_across, both)[0], True)
    message_chip = ring_swap(edge(0, ROWS, left_chip, both)[0], False)
    own_across, own_chip = middle(*own_left, both)
    out = finish(False, 0, BLOCK, own_chip, message_chip)
    out = finish(True, 0, BLOCK // 2, own_across, message_0, out)
    out = finish(True, BLOCK // 2, BLOCK, own_across, message_1, out)
    return out.reshape(2 * ROWS, COLS)


def solution(mesh):
    spec = P(("grp", "blk"), None)
    return jax.shard_map(body, mesh=mesh, in_specs=(spec,) * 6, out_specs=spec, check_vma=False)
```

```python
import functools

import jax
import jax.numpy as jnp
from jax import lax
from jax.experimental import pallas as pl
from jax.experimental.pallas import tpu as pltpu
from jax.sharding import PartitionSpec as P

COLS = 256
BLOCK = 64
EB = 16
CHUNK = 2 * BLOCK
ROWS = EB * BLOCK
GROUP = 32
WHOLE = (ROWS,)
PARTS = (ROWS // 2, ROWS // 2)
FLOOR = 2.0**-110
VMEM = pl.BlockSpec(memory_space=pltpu.VMEM)
SMEM = pl.BlockSpec(memory_space=pltpu.SMEM)
ANY = pl.BlockSpec(memory_space=pl.ANY)


def params():
    return pltpu.CompilerParams(vmem_limit_bytes=40 * 1024 * 1024)


def cost(flops, nbytes):
    return pl.CostEstimate(flops=flops, bytes_accessed=nbytes, transcendentals=0)


def parity():
    return lax.rem(lax.axis_index("grp") * lax.axis_size("blk") + lax.axis_index("blk"), 2)


def partner(own, k, members):
    if members & (members - 1) == 0:
        return lax.bitwise_xor(own, jnp.int32(k))
    return lax.rem(own + k, members)


def step_of(own, sender, members):
    if members & (members - 1) == 0:
        return lax.bitwise_xor(jnp.full_like(sender, own), sender)
    return lax.rem(own - sender + members, members)


def pick_kernel(members, capacity, ids, counts, source, *refs):
    fed, refs = refs[:3], refs[3:]
    picked, held, refs = refs[:members], refs[members : members + 3], refs[members + 3 :]
    blocks, id_list, count_list, sems = refs
    own = lax.axis_index("blk")
    copies = [
        pltpu.make_async_copy(here, there, sems.at[n])
        for n, (here, there) in enumerate(
            zip((ids, counts, source) + fed, (id_list, count_list, blocks) + held)
        )
    ]
    for copy in copies:
        copy.start()
    for copy in copies[:3]:
        copy.wait()
    for k in range(members):
        reader = partner(own, k, members)
        for j in range(capacity):
            start = pl.multiple_of(id_list[0, reader * capacity + j] * BLOCK, BLOCK)
            live = (j < count_list[0, reader]).astype(jnp.float32).astype(jnp.bfloat16)
            picked[k][j * BLOCK : (j + 1) * BLOCK] = blocks[pl.ds(start, BLOCK)] * live
    for copy in copies[3:]:
        copy.wait()


def pick(members, capacity, send_ids, send_counts, source, *fed):
    shape = (capacity * BLOCK, COLS)
    given = [pltpu.with_memory_space_constraint(x, pltpu.HBM) for x in (send_ids, send_counts, source) + fed]
    results = pl.pallas_call(
        functools.partial(pick_kernel, members, capacity),
        out_shape=[pltpu.VMEM(shape, jnp.bfloat16)] * members + [pltpu.VMEM(x.shape, x.dtype) for x in fed],
        in_specs=[ANY] * len(given),
        out_specs=[VMEM] * (members + len(fed)),
        scratch_shapes=[
            pltpu.VMEM(source.shape, source.dtype),
            pltpu.SMEM(send_ids.shape, jnp.int32),
            pltpu.SMEM(send_counts.shape, jnp.int32),
            pltpu.SemaphoreType.DMA((len(given),)),
        ],
        compiler_params=params(),
        name="pick",
    )(*given)
    return results[:members], results[members:]


def spread_kernel(members, capacity, quarters, slots, targets, weights, *outs):
    own = lax.axis_index("blk")
    tiles = weights.shape[0]
    width = members * CHUNK
    count = len(quarters)
    slot = slots[...]
    sender = slot // capacity
    place = step_of(own, sender, members) * capacity + slot % capacity
    target = targets[...]
    rows = lax.broadcasted_iota(jnp.int32, (count * EB, tiles), 0)
    wanted = rows
    for n, (even, odd) in enumerate(quarters):
        wanted = jnp.where(rows // EB == n, rows % EB + jnp.where(parity() == 1, odd, even) * EB, wanted)
    hit = target == wanted
    table = jnp.concatenate(
        [
            jnp.concatenate(
                [(hit & (place == k * capacity + j)).astype(jnp.float32) for j in range(capacity)], axis=1
            )
            for k in range(members)
        ],
        axis=0,
    ).astype(jnp.bfloat16)
    left = (lax.broadcasted_iota(jnp.int32, (1, CHUNK), 1) < BLOCK).astype(jnp.float32)
    low = left.astype(jnp.bfloat16)
    high = (1.0 - left).astype(jnp.bfloat16)

    def step(c, _):
        x = weights[:, pl.ds(pl.multiple_of(c * CHUNK, CHUNK), CHUNK)]
        swapped = jnp.concatenate([x[:, BLOCK:], x[:, :BLOCK]], axis=1)
        right = jnp.concatenate(
            [
                jnp.concatenate([x * low, swapped * low], axis=1),
                jnp.concatenate([swapped * high, x * high], axis=1),
            ],
            axis=0,
        )
        sums = jnp.dot(table, right, preferred_element_type=jnp.float32)
        coarse = sums.astype(jnp.bfloat16)
        fine = (sums - coarse.astype(jnp.float32)).astype(jnp.bfloat16)
        for k in range(members):
            for n in range(count):
                top = (k * count + n) * EB
                for h in range(2):
                    row = pl.ds(pl.multiple_of((2 * c + h) * EB, EB), EB)
                    part = (slice(top, top + EB), slice(h * CHUNK, (h + 1) * CHUNK))
                    outs[n][row, k * CHUNK : (k + 1) * CHUNK] = coarse[part]
                    outs[n][row, width + k * CHUNK : width + (k + 1) * CHUNK] = fine[part]
        return 0

    lax.fori_loop(0, BLOCK // 2, step, 0, unroll=8)


def spread(members, capacity, quarters, slots, targets, weights):
    shape = (ROWS, 2 * members * CHUNK)
    tiles = weights.shape[0]
    return pl.pallas_call(
        functools.partial(spread_kernel, members, capacity, quarters),
        out_shape=[pltpu.VMEM(shape, jnp.bfloat16)] * len(quarters),
        in_specs=[VMEM] * 3,
        out_specs=[VMEM] * len(quarters),
        compiler_params=params(),
        cost_estimate=cost(2 * members * EB * len(quarters) * 2 * tiles * 8192, 6 * 2**20),
        name="spread",
    )(slots, targets, weights)


def stack_kernel(blocks, both):
    rows = blocks[0].shape[0]
    for half in range(2):
        for k, block in enumerate(blocks):
            start = (half * len(blocks) + k) * rows
            both[start : start + rows] = block[...]


def coded(left, first, count, both, message, powers):
    step = min(count, 256)
    for start in range(0, count, step):
        rows = left[first + start : first + start + step]
        piece = jnp.dot(rows, both[...], preferred_element_type=jnp.float32)
        for g in range(step // GROUP):
            rows = piece[g * GROUP : (g + 1) * GROUP]
            most = jnp.maximum(jnp.max(jnp.abs(rows), axis=0, keepdims=True), FLOOR)
            power = jnp.floor(jnp.log2(most) + 0.001) + 1.0
            whole = jnp.round(rows * jnp.exp2(15.0 - power)).astype(jnp.int32)
            message[start + g * GROUP : start + (g + 1) * GROUP] = whole.astype(jnp.int16)
            at = start // GROUP + g
            powers[at : at + 1] = power.astype(jnp.int32)
    message[count : count + count // GROUP] = powers[...].astype(jnp.int16)


def edge_kernel(parts, blocks, left, *refs):
    received, refs = refs[:blocks], refs[blocks:]
    messages, refs = refs[: len(parts)], refs[len(parts) :]
    both, powers = refs[0], refs[1:]
    if blocks > 1:
        stack_kernel(received, both)
    else:
        both, powers = received[0], refs
    first = 0
    for count, message, power in zip(parts, messages, powers):
        coded(left, first, count, both, message, power)
        first += count


def edge(parts, left, *right):
    out_shape = [pltpu.VMEM((count + count // GROUP, COLS), jnp.int16) for count in parts]
    if len(right) > 1:
        out_shape.append(pltpu.VMEM((left.shape[1], COLS), jnp.bfloat16))
    return pl.pallas_call(
        functools.partial(edge_kernel, parts, len(right)),
        out_shape=out_shape,
        in_specs=[VMEM] * (1 + len(right)),
        out_specs=[VMEM] * len(out_shape),
        scratch_shapes=[pltpu.VMEM((count // GROUP, COLS), jnp.int32) for count in parts],
        compiler_params=params(),
        cost_estimate=cost(2 * ROWS * left.shape[1] * COLS, 2 * 2**20),
        name="edge",
    )(left, *right)


def middle_kernel(first, second, both, *outs):
    step = 256
    for left, out in zip((first, second), outs):
        for start in range(0, ROWS, step):
            out[start : start + step] = jnp.dot(
                left[start : start + step], both[...], preferred_element_type=jnp.float32
            )


def middle(first, second, both):
    return pl.pallas_call(
        middle_kernel,
        out_shape=[pltpu.VMEM((ROWS, COLS), jnp.float32)] * 2,
        in_specs=[VMEM] * 3,
        out_specs=[VMEM] * 2,
        compiler_params=params(),
        cost_estimate=cost(4 * ROWS * first.shape[1] * COLS, 4 * 2**20),
        name="middle",
    )(first, second, both)


def finish_kernel(across, parts, own, *refs):
    messages, (out, rows, sems) = refs[: len(parts)], refs[-3:]
    half = parity() if across else 1 - parity()
    pitch = BLOCK + 8
    targets = rows.reshape(COLS // 128, EB, pitch, 128)
    some = EB // 2
    copies = []
    for first in range(0, EB, some):
        i = 0
        for count, message in zip(parts, messages):
            scale = jnp.exp2(message[count : count + count // GROUP].astype(jnp.float32) - 15.0)
            for at in range(0, count, EB):
                g = at // GROUP
                value = message[at : at + EB].astype(jnp.float32)[first : first + some]
                value = own[i * EB + first : i * EB + first + some] + value * scale[g : g + 1]
                for n in range(COLS // 128):
                    place = pl.ds(first * pitch + i, some, stride=pitch)
                    rows[n, place] = value[:, n * 128 : (n + 1) * 128]
                i += 1
        for n in range(COLS // 128):
            here = targets.at[n, pl.ds(first, some), pl.ds(0, BLOCK)]
            there = out.at[pl.ds(half * EB + first, some), :, pl.ds(n * 128, 128)]
            copies.append(pltpu.make_async_copy(here, there, sems.at[len(copies)]))
            copies[-1].start()
    for copy in copies:
        copy.wait()


def finish(across, parts, own, messages, out=None):
    given = [] if out is None else [out]
    return pl.pallas_call(
        functools.partial(finish_kernel, across, parts),
        out_shape=jax.ShapeDtypeStruct((2 * EB, BLOCK, COLS), jnp.float32),
        in_specs=[VMEM] * (1 + len(parts)) + [ANY] * len(given),
        out_specs=ANY,
        scratch_shapes=[
            pltpu.VMEM((COLS // 128, EB * (BLOCK + 8), 128), jnp.float32),
            pltpu.SemaphoreType.DMA((2 * COLS // 128,)),
        ],
        input_output_aliases={} if out is None else {1 + len(parts): 0},
        compiler_params=params(),
        cost_estimate=cost(3 * ROWS * COLS, 2 * 2**20),
        name="finish",
    )(own, *messages, *given)


def passed_along(shard, axis, by):
    count = lax.axis_size(axis)
    return lax.ppermute(shard, axis, [(i, (i + by) % count) for i in range(count)])


def exchanged(shard, k):
    members = lax.axis_size("blk")
    if members & (members - 1) == 0:
        return lax.ppermute(shard, "blk", [(i, i ^ k) for i in range(members)])
    return passed_along(shard, "blk", k)


def ring_swap(shard, across):
    axes = ("grp", "blk")
    count = lax.axis_size(axes)
    if across:
        return lax.ppermute(shard, axes, [(i, (i + (1 if i % 2 else -1)) % count) for i in range(count)])
    return lax.ppermute(shard, axes, [(i, i ^ 1) for i in range(count)])


def body(source, send_ids, send_counts, tile_slot, tile_target, tile_weights):
    members = lax.axis_size("blk")
    capacity = send_ids.shape[1] // members
    picked, tiles = pick(
        members, capacity, send_ids, send_counts, source, tile_slot, tile_target, tile_weights
    )
    blocks = [picked[0]] + [exchanged(picked[k], k) for k in range(1, members)]
    left_across, left_chip = spread(members, capacity, ((0, 3), (3, 0)), *tiles)
    message_across, both = edge(WHOLE, left_across, *blocks)
    message_across = ring_swap(message_across, True)
    messages_chip = [ring_swap(message, False) for message in edge(PARTS, left_chip, both)]
    tiles, both = lax.optimization_barrier((tiles, both))
    own_left = spread(members, capacity, ((1, 2), (2, 1)), *tiles)
    own_across, own_chip = middle(*own_left, both)
    out = finish(False, PARTS, own_chip, messages_chip)
    out = finish(True, WHOLE, own_across, [message_across], out)
    return out.reshape(2 * ROWS, COLS)


def solution(mesh):
    spec = P(("grp", "blk"), None)
    return jax.shard_map(body, mesh=mesh, in_specs=(spec,) * 6, out_specs=spec, check_vma=False)
```

```python
import functools

import jax
import jax.numpy as jnp
from jax import lax
from jax.experimental import pallas as pl
from jax.experimental.pallas import tpu as pltpu
from jax.sharding import PartitionSpec as P

COLS = 256
BLOCK = 64
EB = 16
CHUNK = 2 * BLOCK
ROWS = EB * BLOCK
GROUP = 32
EARLY = 2
SLABS = 4
WHOLE = (ROWS,)
PARTS = (ROWS // 2, ROWS // 2)
FLOOR = 2.0**-110
VMEM = pl.BlockSpec(memory_space=pltpu.VMEM)
SMEM = pl.BlockSpec(memory_space=pltpu.SMEM)
ANY = pl.BlockSpec(memory_space=pl.ANY)


def params():
    return pltpu.CompilerParams(vmem_limit_bytes=40 * 1024 * 1024)


def cost(flops, nbytes):
    return pl.CostEstimate(flops=flops, bytes_accessed=nbytes, transcendentals=0)


def parity():
    return lax.rem(lax.axis_index("grp") * lax.axis_size("blk") + lax.axis_index("blk"), 2)


def partner(own, k, members):
    if members & (members - 1) == 0:
        return lax.bitwise_xor(own, jnp.int32(k))
    return lax.rem(own + k, members)


def step_of(own, sender, members):
    if members & (members - 1) == 0:
        return lax.bitwise_xor(jnp.full_like(sender, own), sender)
    return lax.rem(own - sender + members, members)


def pick_kernel(members, capacity, ids, counts, source, *refs):
    picked, (blocks, id_list, count_list, sems) = refs[:members], refs[members:]
    own = lax.axis_index("blk")
    copies = [
        pltpu.make_async_copy(here, there, sems.at[n])
        for n, (here, there) in enumerate(((ids, id_list), (counts, count_list), (source, blocks)))
    ]
    for copy in copies:
        copy.start()
    for copy in copies:
        copy.wait()
    for k in range(members):
        reader = partner(own, k, members)
        for j in range(capacity):
            start = pl.multiple_of(id_list[0, reader * capacity + j] * BLOCK, BLOCK)
            live = (j < count_list[0, reader]).astype(jnp.float32).astype(jnp.bfloat16)
            picked[k][j * BLOCK : (j + 1) * BLOCK] = blocks[pl.ds(start, BLOCK)] * live


def in_hbm(*arrays):
    return [pltpu.with_memory_space_constraint(x, pltpu.HBM) for x in arrays]


def pick(members, capacity, send_ids, send_counts, source):
    shape = (capacity * BLOCK, COLS)
    return pl.pallas_call(
        functools.partial(pick_kernel, members, capacity),
        out_shape=[pltpu.VMEM(shape, jnp.bfloat16)] * members,
        in_specs=[ANY] * 3,
        out_specs=[VMEM] * members,
        scratch_shapes=[
            pltpu.VMEM(source.shape, source.dtype),
            pltpu.SMEM(send_ids.shape, jnp.int32),
            pltpu.SMEM(send_counts.shape, jnp.int32),
            pltpu.SemaphoreType.DMA((3,)),
        ],
        compiler_params=params(),
        name="pick",
    )(*in_hbm(send_ids, send_counts, source))


def lanes_of(k, members):
    if k < EARLY:
        return k * CHUNK, (EARLY + k) * CHUNK
    return (EARLY + k) * CHUNK, (members + k) * CHUNK


def spread_kernel(members, capacity, quarters, *refs):
    here, outs, (slots, targets, weights, sems) = refs[:3], refs[3:-4], refs[-4:]
    slab = weights.shape[1] // SLABS
    copies = [pltpu.make_async_copy(here[n], (slots, targets)[n], sems.at[n]) for n in range(2)]
    for n in range(SLABS):
        part = (slice(None), pl.ds(n * slab, slab))
        copies.append(pltpu.make_async_copy(here[2].at[part], weights.at[part], sems.at[2 + n]))
    for copy in copies:
        copy.start()
    for copy in copies[:2]:
        copy.wait()
    own = lax.axis_index("blk")
    tiles = weights.shape[0]
    count = len(quarters)
    slot = slots[...]
    sender = slot // capacity
    place = step_of(own, sender, members) * capacity + slot % capacity
    target = targets[...]
    rows = lax.broadcasted_iota(jnp.int32, (count * EB, tiles), 0)
    wanted = rows
    for n, (even, odd) in enumerate(quarters):
        wanted = jnp.where(rows // EB == n, rows % EB + jnp.where(parity() == 1, odd, even) * EB, wanted)
    hit = target == wanted
    table = jnp.concatenate(
        [
            jnp.concatenate(
                [(hit & (place == k * capacity + j)).astype(jnp.float32) for j in range(capacity)], axis=1
            )
            for k in range(members)
        ],
        axis=0,
    ).astype(jnp.bfloat16)
    left = (lax.broadcasted_iota(jnp.int32, (1, CHUNK), 1) < BLOCK).astype(jnp.float32)
    low = left.astype(jnp.bfloat16)
    high = (1.0 - left).astype(jnp.bfloat16)

    def step(c, _):
        x = weights[:, pl.ds(pl.multiple_of(c * CHUNK, CHUNK), CHUNK)]
        swapped = jnp.concatenate([x[:, BLOCK:], x[:, :BLOCK]], axis=1)
        right = jnp.concatenate(
            [
                jnp.concatenate([x * low, swapped * low], axis=1),
                jnp.concatenate([swapped * high, x * high], axis=1),
            ],
            axis=0,
        )
        sums = jnp.dot(table, right, preferred_element_type=jnp.float32)
        coarse = sums.astype(jnp.bfloat16)
        fine = (sums - coarse.astype(jnp.float32)).astype(jnp.bfloat16)
        for k in range(members):
            for n in range(count):
                top = (k * count + n) * EB
                for h in range(2):
                    row = pl.ds(pl.multiple_of((2 * c + h) * EB, EB), EB)
                    part = (slice(top, top + EB), slice(h * CHUNK, (h + 1) * CHUNK))
                    for lanes, value in zip(lanes_of(k, members), (coarse, fine)):
                        outs[n][row, lanes : lanes + CHUNK] = value[part]
        return 0

    each = slab // CHUNK
    for n in range(SLABS):
        copies[2 + n].wait()
        lax.fori_loop(n * each, (n + 1) * each, step, 0, unroll=each)


def spread(members, capacity, quarters, slots, targets, weights):
    shape = (ROWS, 2 * members * CHUNK)
    tiles = weights.shape[0]
    return pl.pallas_call(
        functools.partial(spread_kernel, members, capacity, quarters),
        out_shape=[pltpu.VMEM(shape, jnp.bfloat16)] * len(quarters),
        in_specs=[ANY] * 3,
        out_specs=[VMEM] * len(quarters),
        scratch_shapes=[
            pltpu.VMEM(slots.shape, jnp.int32),
            pltpu.VMEM(targets.shape, jnp.int32),
            pltpu.VMEM(weights.shape, weights.dtype),
            pltpu.SemaphoreType.DMA((2 + SLABS,)),
        ],
        compiler_params=params(),
        cost_estimate=cost(2 * members * EB * len(quarters) * 2 * tiles * 8192, 6 * 2**20),
        name="spread",
    )(*in_hbm(slots, targets, weights))


def stacked(blocks, both):
    rows = blocks[0].shape[0]
    for half in range(2):
        for k, block in enumerate(blocks):
            start = (half * len(blocks) + k) * rows
            both[start : start + rows] = block[...]


def early_kernel(left, *refs):
    blocks, (sums, both) = refs[:-2], refs[-2:]
    stacked(blocks, both)
    sums[...] = jnp.dot(left[:, : both.shape[0]], both[...], preferred_element_type=jnp.float32)


def early(left, blocks):
    depth = 2 * EARLY * CHUNK
    return pl.pallas_call(
        early_kernel,
        out_shape=[pltpu.VMEM((ROWS, COLS), jnp.float32), pltpu.VMEM((depth, COLS), jnp.bfloat16)],
        in_specs=[VMEM] * (1 + len(blocks)),
        out_specs=[VMEM] * 2,
        compiler_params=params(),
        cost_estimate=cost(2 * ROWS * depth * COLS, 2 * 2**20),
        name="early",
    )(left, *blocks)


def coded(piece, message, powers):
    count = piece.shape[0]
    for g in range(count // GROUP):
        rows = piece[g * GROUP : (g + 1) * GROUP]
        most = jnp.maximum(jnp.max(jnp.abs(rows), axis=0, keepdims=True), FLOOR)
        power = jnp.floor(jnp.log2(most) + 0.001) + 1.0
        whole = jnp.round(rows * jnp.exp2(15.0 - power)).astype(jnp.int32)
        message[g * GROUP : (g + 1) * GROUP] = whole.astype(jnp.int16)
        powers[g : g + 1] = power.astype(jnp.int32)
    message[count : count + count // GROUP] = powers[...].astype(jnp.int16)


def product(left, first, later):
    both = jnp.concatenate([first[...], later[...]], axis=0)
    return jnp.dot(left, both, preferred_element_type=jnp.float32)


def across_kernel(left, sums, *refs):
    blocks, (message, both, powers) = refs[:-3], refs[-3:]
    stacked(blocks, both)
    start = left.shape[1] - both.shape[0]
    piece = jnp.dot(left[:, start:], both[...], preferred_element_type=jnp.float32)
    coded(sums[...] + piece, message, powers)


def message_of(count):
    return pltpu.VMEM((count + count // GROUP, COLS), jnp.int16)


def powers_of(count):
    return pltpu.VMEM((count // GROUP, COLS), jnp.int32)


def across_edge(left, sums, blocks):
    depth = 2 * len(blocks) * CHUNK
    return pl.pallas_call(
        across_kernel,
        out_shape=[message_of(ROWS), pltpu.VMEM((depth, COLS), jnp.bfloat16)],
        in_specs=[VMEM] * (2 + len(blocks)),
        out_specs=[VMEM] * 2,
        scratch_shapes=[powers_of(ROWS)],
        compiler_params=params(),
        cost_estimate=cost(2 * ROWS * depth * COLS, 2 * 2**20),
        name="across",
    )(left, sums, *blocks)


def chip_kernel(parts, left, first, later, *refs):
    start = 0
    for count, message, powers in zip(parts, refs[: len(parts)], refs[len(parts) :]):
        coded(product(left[start : start + count], first, later), message, powers)
        start += count


def chip_edge(parts, left, first, later):
    return pl.pallas_call(
        functools.partial(chip_kernel, parts),
        out_shape=[message_of(count) for count in parts],
        in_specs=[VMEM] * 3,
        out_specs=[VMEM] * len(parts),
        scratch_shapes=[powers_of(count) for count in parts],
        compiler_params=params(),
        cost_estimate=cost(2 * ROWS * left.shape[1] * COLS, 2 * 2**20),
        name="chip",
    )(left, first, later)


def middle_kernel(left_0, left_1, first, later, *outs):
    step = 256
    for left, out in zip((left_0, left_1), outs):
        for start in range(0, ROWS, step):
            out[start : start + step] = product(left[start : start + step], first, later)


def middle(left_0, left_1, first, later):
    return pl.pallas_call(
        middle_kernel,
        out_shape=[pltpu.VMEM((ROWS, COLS), jnp.float32)] * 2,
        in_specs=[VMEM] * 4,
        out_specs=[VMEM] * 2,
        compiler_params=params(),
        cost_estimate=cost(4 * ROWS * left_0.shape[1] * COLS, 4 * 2**20),
        name="middle",
    )(left_0, left_1, first, later)


def finish_kernel(across, parts, own, *refs):
    messages, (out, rows, sems) = refs[: len(parts)], refs[-3:]
    half = parity() if across else 1 - parity()
    pitch = BLOCK + 8
    targets = rows.reshape(COLS // 128, EB, pitch, 128)
    some = EB // 2
    copies = []
    for first in range(0, EB, some):
        i = 0
        for count, message in zip(parts, messages):
            scale = jnp.exp2(message[count : count + count // GROUP].astype(jnp.float32) - 15.0)
            for at in range(0, count, EB):
                g = at // GROUP
                value = message[at : at + EB].astype(jnp.float32)[first : first + some]
                value = own[i * EB + first : i * EB + first + some] + value * scale[g : g + 1]
                for n in range(COLS // 128):
                    place = pl.ds(first * pitch + i, some, stride=pitch)
                    rows[n, place] = value[:, n * 128 : (n + 1) * 128]
                i += 1
        for n in range(COLS // 128):
            here = targets.at[n, pl.ds(first, some), pl.ds(0, BLOCK)]
            there = out.at[pl.ds(half * EB + first, some), :, pl.ds(n * 128, 128)]
            copies.append(pltpu.make_async_copy(here, there, sems.at[len(copies)]))
            copies[-1].start()
    for copy in copies:
        copy.wait()


def finish(across, parts, own, messages, out=None):
    given = [] if out is None else [out]
    return pl.pallas_call(
        functools.partial(finish_kernel, across, parts),
        out_shape=jax.ShapeDtypeStruct((2 * EB, BLOCK, COLS), jnp.float32),
        in_specs=[VMEM] * (1 + len(parts)) + [ANY] * len(given),
        out_specs=ANY,
        scratch_shapes=[
            pltpu.VMEM((COLS // 128, EB * (BLOCK + 8), 128), jnp.float32),
            pltpu.SemaphoreType.DMA((2 * COLS // 128,)),
        ],
        input_output_aliases={} if out is None else {1 + len(parts): 0},
        compiler_params=params(),
        cost_estimate=cost(3 * ROWS * COLS, 2 * 2**20),
        name="finish",
    )(own, *messages, *given)


def passed_along(shard, axis, by):
    count = lax.axis_size(axis)
    return lax.ppermute(shard, axis, [(i, (i + by) % count) for i in range(count)])


def exchanged(shard, k):
    members = lax.axis_size("blk")
    if members & (members - 1) == 0:
        return lax.ppermute(shard, "blk", [(i, i ^ k) for i in range(members)])
    return passed_along(shard, "blk", k)


def ring_swap(shard, across):
    axes = ("grp", "blk")
    count = lax.axis_size(axes)
    if across:
        return lax.ppermute(shard, axes, [(i, (i + (1 if i % 2 else -1)) % count) for i in range(count)])
    return lax.ppermute(shard, axes, [(i, i ^ 1) for i in range(count)])


def body(source, send_ids, send_counts, tile_slot, tile_target, tile_weights):
    members = lax.axis_size("blk")
    capacity = send_ids.shape[1] // members
    picked = pick(members, capacity, send_ids, send_counts, source)
    later_blocks = [exchanged(picked[k], k) for k in range(EARLY, members)]
    early_blocks = [picked[0]] + [exchanged(picked[k], k) for k in range(1, EARLY)]
    tiles = (tile_slot, tile_target, tile_weights)
    left_across, left_chip = spread(members, capacity, ((0, 3), (3, 0)), *tiles)
    sums, first = early(left_across, early_blocks)
    message_across, later = across_edge(left_across, sums, later_blocks)
    message_across = ring_swap(message_across, True)
    messages_chip = [ring_swap(message, False) for message in chip_edge(PARTS, left_chip, first, later)]
    tiles, later = lax.optimization_barrier((tiles, later))
    own_left = spread(members, capacity, ((1, 2), (2, 1)), *tiles)
    own_across, own_chip = middle(*own_left, first, later)
    out = finish(False, PARTS, own_chip, messages_chip)
    out = finish(True, WHOLE, own_across, [message_across], out)
    return out.reshape(2 * ROWS, COLS)


def solution(mesh):
    spec = P(("grp", "blk"), None)
    return jax.shard_map(body, mesh=mesh, in_specs=(spec,) * 6, out_specs=spec, check_vma=False)
```

```python
import functools

import jax
import jax.numpy as jnp
from jax import lax
from jax.experimental import pallas as pl
from jax.experimental.pallas import tpu as pltpu
from jax.sharding import PartitionSpec as P

COLS = 256
BLOCK = 64
EB = 16
CHUNK = 2 * BLOCK
ROWS = EB * BLOCK
GROUP = 64
EARLY = 2
SLABS = 4
RING = ("grp", "blk")
WHOLE = (ROWS,)
PARTS = (ROWS // 2, ROWS // 2)
FLOOR = 2.0**-110
VMEM = pl.BlockSpec(memory_space=pltpu.VMEM)
SMEM = pl.BlockSpec(memory_space=pltpu.SMEM)
ANY = pl.BlockSpec(memory_space=pl.ANY)


def params():
    return pltpu.CompilerParams(vmem_limit_bytes=40 * 1024 * 1024)


def cost(flops, nbytes):
    return pl.CostEstimate(flops=flops, bytes_accessed=nbytes, transcendentals=0)


def parity():
    return lax.rem(lax.axis_index("grp") * lax.axis_size("blk") + lax.axis_index("blk"), 2)


def partner(own, k, members):
    if members & (members - 1) == 0:
        return lax.bitwise_xor(own, jnp.int32(k))
    return lax.rem(own + k, members)


def step_of(own, sender, members):
    if members & (members - 1) == 0:
        return lax.bitwise_xor(jnp.full_like(sender, own), sender)
    return lax.rem(own - sender + members, members)


def pick_kernel(members, capacity, ids, counts, source, *refs):
    picked, (blocks, id_list, count_list, sems) = list(refs[:-4]), refs[-4:]
    own = lax.axis_index("blk")
    copies = [
        pltpu.make_async_copy(here, there, sems.at[n])
        for n, (here, there) in enumerate(((ids, id_list), (counts, count_list), (source, blocks)))
    ]
    for copy in copies:
        copy.start()
    for copy in copies:
        copy.wait()
    at = 0
    for k in range(members):
        reader = partner(own, k, members)
        for j in range(capacity):
            start = pl.multiple_of(id_list[0, reader * capacity + j] * BLOCK, BLOCK)
            live = (j < count_list[0, reader]).astype(jnp.float32).astype(jnp.bfloat16)
            if at == picked[0].shape[0]:
                picked.pop(0)
                at = 0
            picked[0][at : at + BLOCK] = blocks[pl.ds(start, BLOCK)] * live
            at += BLOCK


def in_hbm(*arrays):
    return [pltpu.with_memory_space_constraint(x, pltpu.HBM) for x in arrays]


def pick(members, capacity, send_ids, send_counts, source):
    whole = pltpu.VMEM((capacity * BLOCK, COLS), jnp.bfloat16)
    single = pltpu.VMEM((BLOCK, COLS), jnp.bfloat16)
    out_shape = [whole] + [single] * (EARLY - 1) * capacity + [whole] * (members - EARLY)
    return pl.pallas_call(
        functools.partial(pick_kernel, members, capacity),
        out_shape=out_shape,
        in_specs=[ANY] * 3,
        out_specs=[VMEM] * len(out_shape),
        scratch_shapes=[
            pltpu.VMEM(source.shape, source.dtype),
            pltpu.SMEM(send_ids.shape, jnp.int32),
            pltpu.SMEM(send_counts.shape, jnp.int32),
            pltpu.SemaphoreType.DMA((3,)),
        ],
        compiler_params=params(),
        name="pick",
    )(*in_hbm(send_ids, send_counts, source))


def lanes_of(k, members):
    if k < EARLY:
        return k * CHUNK, (EARLY + k) * CHUNK
    return (EARLY + k) * CHUNK, (members + k) * CHUNK


def spread_kernel(members, capacity, quarters, *refs):
    here, outs, (slots, targets, weights, sems) = refs[:3], refs[3:-4], refs[-4:]
    slab = weights.shape[1] // SLABS
    copies = [pltpu.make_async_copy(here[n], (slots, targets)[n], sems.at[n]) for n in range(2)]
    for n in range(SLABS):
        part = (slice(None), pl.ds(n * slab, slab))
        copies.append(pltpu.make_async_copy(here[2].at[part], weights.at[part], sems.at[2 + n]))
    for copy in copies:
        copy.start()
    for copy in copies[:2]:
        copy.wait()
    own = lax.axis_index("blk")
    tiles = weights.shape[0]
    count = len(quarters)
    slot = slots[...]
    sender = slot // capacity
    place = step_of(own, sender, members) * capacity + slot % capacity
    target = targets[...]
    rows = lax.broadcasted_iota(jnp.int32, (count * EB, tiles), 0)
    wanted = rows
    for n, (even, odd) in enumerate(quarters):
        wanted = jnp.where(rows // EB == n, rows % EB + jnp.where(parity() == 1, odd, even) * EB, wanted)
    hit = target == wanted
    table = jnp.concatenate(
        [
            jnp.concatenate(
                [(hit & (place == k * capacity + j)).astype(jnp.float32) for j in range(capacity)], axis=1
            )
            for k in range(members)
        ],
        axis=0,
    ).astype(jnp.bfloat16)
    left = (lax.broadcasted_iota(jnp.int32, (1, CHUNK), 1) < BLOCK).astype(jnp.float32)
    low = left.astype(jnp.bfloat16)
    high = (1.0 - left).astype(jnp.bfloat16)

    def step(c, _):
        x = weights[:, pl.ds(pl.multiple_of(c * CHUNK, CHUNK), CHUNK)]
        swapped = jnp.concatenate([x[:, BLOCK:], x[:, :BLOCK]], axis=1)
        right = jnp.concatenate(
            [
                jnp.concatenate([x * low, swapped * low], axis=1),
                jnp.concatenate([swapped * high, x * high], axis=1),
            ],
            axis=0,
        )
        sums = jnp.dot(table, right, preferred_element_type=jnp.float32)
        coarse = sums.astype(jnp.bfloat16)
        fine = (sums - coarse.astype(jnp.float32)).astype(jnp.bfloat16)
        for k in range(members):
            for n in range(count):
                top = (k * count + n) * EB
                for h in range(2):
                    row = pl.ds(pl.multiple_of((2 * c + h) * EB, EB), EB)
                    part = (slice(top, top + EB), slice(h * CHUNK, (h + 1) * CHUNK))
                    for lanes, value in zip(lanes_of(k, members), (coarse, fine)):
                        outs[n][row, lanes : lanes + CHUNK] = value[part]
        return 0

    each = slab // CHUNK
    for n in range(SLABS):
        copies[2 + n].wait()
        lax.fori_loop(n * each, (n + 1) * each, step, 0, unroll=each)


def spread(members, capacity, quarters, slots, targets, weights):
    shape = (ROWS, 2 * members * CHUNK)
    tiles = weights.shape[0]
    return pl.pallas_call(
        functools.partial(spread_kernel, members, capacity, quarters),
        out_shape=[pltpu.VMEM(shape, jnp.bfloat16)] * len(quarters),
        in_specs=[ANY] * 3,
        out_specs=[VMEM] * len(quarters),
        scratch_shapes=[
            pltpu.VMEM(slots.shape, jnp.int32),
            pltpu.VMEM(targets.shape, jnp.int32),
            pltpu.VMEM(weights.shape, weights.dtype),
            pltpu.SemaphoreType.DMA((2 + SLABS,)),
        ],
        compiler_params=params(),
        cost_estimate=cost(2 * members * EB * len(quarters) * 2 * tiles * 8192, 6 * 2**20),
        name="spread",
    )(*in_hbm(slots, targets, weights))


def stacked(blocks, both):
    start = 0
    for block in 2 * blocks:
        both[start : start + block.shape[0]] = block[...]
        start += block.shape[0]


def early_kernel(left, *refs):
    blocks, (sums, both) = refs[:-2], refs[-2:]
    stacked(blocks, both)
    sums[...] = jnp.dot(left[:, : both.shape[0]], both[...], preferred_element_type=jnp.float32)


def early(left, blocks):
    depth = 2 * EARLY * CHUNK
    return pl.pallas_call(
        early_kernel,
        out_shape=[pltpu.VMEM((ROWS, COLS), jnp.float32), pltpu.VMEM((depth, COLS), jnp.bfloat16)],
        in_specs=[VMEM] * (1 + len(blocks)),
        out_specs=[VMEM] * 2,
        compiler_params=params(),
        cost_estimate=cost(0, 2**10),
        name="early",
    )(left, *blocks)


def coded(piece, message, powers):
    count = piece.shape[0]
    if count // GROUP < powers.shape[0]:
        powers[...] = jnp.zeros_like(powers)
    for g in range(count // GROUP):
        rows = piece[g * GROUP : (g + 1) * GROUP]
        most = jnp.maximum(jnp.max(jnp.abs(rows), axis=0, keepdims=True), FLOOR)
        power = jnp.floor(jnp.log2(most) + 0.001) + 1.0
        whole = jnp.round(rows * jnp.exp2(15.0 - power)).astype(jnp.int32)
        message[g * GROUP : (g + 1) * GROUP] = whole.astype(jnp.int16)
        powers[g : g + 1] = power.astype(jnp.int32)
    message[count : count + powers.shape[0]] = powers[...].astype(jnp.int16)


def product(left, first, later):
    both = jnp.concatenate([first[...], later[...]], axis=0)
    return jnp.dot(left, both, preferred_element_type=jnp.float32)


def send_kernel(odd, left, sums, *refs):
    blocks, message, refs = refs[: -3 if odd else -2], refs[-3 if odd else -2], refs[-2 if odd else -1 :]
    if odd:
        both, powers = refs
        stacked(blocks, both)
    else:
        both, powers = blocks[0], refs[0]

    @pl.when(parity() == (1 if odd else 0))
    def _():
        start = left.shape[1] - both.shape[0]
        piece = jnp.dot(left[:, start:], both[...], preferred_element_type=jnp.float32)
        coded(sums[...] + piece, message, powers)


def scales(count):
    return max(count // GROUP, 16)


def message_of(count):
    return pltpu.VMEM((count + scales(count), COLS), jnp.int16)


def powers_of(count):
    return pltpu.VMEM((scales(count), COLS), jnp.int32)


def send_edge(odd, left, sums, *blocks):
    depth = 2 * sum(block.shape[0] for block in blocks) if odd else blocks[0].shape[0]
    out_shape = [message_of(ROWS)]
    if odd:
        out_shape.append(pltpu.VMEM((depth, COLS), jnp.bfloat16))
    return pl.pallas_call(
        functools.partial(send_kernel, odd),
        out_shape=out_shape,
        in_specs=[VMEM] * (2 + len(blocks)),
        out_specs=[VMEM] * len(out_shape),
        scratch_shapes=[powers_of(ROWS)],
        compiler_params=params(),
        cost_estimate=cost(2 * ROWS * depth * COLS, 2 * 2**20),
        name="send_odd" if odd else "send_even",
    )(left, sums, *blocks)


def chip_kernel(parts, left, first, later, *refs):
    start = 0
    for count, message, powers in zip(parts, refs[: len(parts)], refs[len(parts) :]):
        coded(product(left[start : start + count], first, later), message, powers)
        start += count


def chip_edge(parts, left, first, later):
    return pl.pallas_call(
        functools.partial(chip_kernel, parts),
        out_shape=[message_of(count) for count in parts],
        in_specs=[VMEM] * 3,
        out_specs=[VMEM] * len(parts),
        scratch_shapes=[powers_of(count) for count in parts],
        compiler_params=params(),
        cost_estimate=cost(2 * ROWS * left.shape[1] * COLS, 2 * 2**20),
        name="chip",
    )(left, first, later)


def middle_kernel(left_0, left_1, first, later, *outs):
    step = 256
    for left, out in zip((left_0, left_1), outs):
        for start in range(0, ROWS, step):
            out[start : start + step] = product(left[start : start + step], first, later)


def middle(left_0, left_1, first, later):
    return pl.pallas_call(
        middle_kernel,
        out_shape=[pltpu.VMEM((ROWS, COLS), jnp.float32)] * 2,
        in_specs=[VMEM] * 4,
        out_specs=[VMEM] * 2,
        compiler_params=params(),
        cost_estimate=cost(4 * ROWS * left_0.shape[1] * COLS, 4 * 2**20),
        name="middle",
    )(left_0, left_1, first, later)


def finish_half(half, parts, own, messages, out, rows, sems):
    pitch = BLOCK + 8
    targets = rows.reshape(COLS // 128, EB, pitch, 128)
    some = EB // 2
    copies = []
    for first in range(0, EB, some):
        i = 0
        for count, message in zip(parts, messages):
            scale = jnp.exp2(message[count : count + scales(count)].astype(jnp.float32) - 15.0)
            for at in range(0, count, EB):
                g = at // GROUP
                value = message[at : at + EB].astype(jnp.float32)[first : first + some]
                value = own[i * EB + first : i * EB + first + some] + value * scale[g : g + 1]
                for n in range(COLS // 128):
                    place = pl.ds(first * pitch + i, some, stride=pitch)
                    rows[n, place] = value[:, n * 128 : (n + 1) * 128]
                i += 1
        for n in range(COLS // 128):
            here = targets.at[n, pl.ds(first, some), pl.ds(0, BLOCK)]
            there = out.at[pl.ds(half * EB + first, some), :, pl.ds(n * 128, 128)]
            copies.append(pltpu.make_async_copy(here, there, sems.at[len(copies)]))
            copies[-1].start()
    for copy in copies:
        copy.wait()


def finish_kernel(role, parts, own, *refs):
    messages, rest = refs[: len(parts)], refs[-3:]
    if role is None:
        finish_half(1 - parity(), parts, own, messages, *rest)
        return

    @pl.when(parity() == role)
    def _():
        finish_half(role, parts, own, messages, *rest)


def finish(role, parts, own, messages, out=None):
    given = [] if out is None else [out]
    return pl.pallas_call(
        functools.partial(finish_kernel, role, parts),
        out_shape=jax.ShapeDtypeStruct((2 * EB, BLOCK, COLS), jnp.float32),
        in_specs=[VMEM] * (1 + len(parts)) + [ANY] * len(given),
        out_specs=ANY,
        scratch_shapes=[
            pltpu.VMEM((COLS // 128, EB * (BLOCK + 8), 128), jnp.float32),
            pltpu.SemaphoreType.DMA((2 * COLS // 128,)),
        ],
        input_output_aliases={} if out is None else {1 + len(parts): 0},
        compiler_params=params(),
        cost_estimate=cost(3 * ROWS * COLS, 2 * 2**20),
        name="finish",
    )(own, *messages, *given)


def passed_along(shard, axis, by):
    count = lax.axis_size(axis)
    return lax.ppermute(shard, axis, [(i, (i + by) % count) for i in range(count)])


def exchanged(shard, k):
    members = lax.axis_size("blk")
    if members & (members - 1) == 0:
        return lax.ppermute(shard, "blk", [(i, i ^ k) for i in range(members)])
    return passed_along(shard, "blk", k)


def ring_pairs():
    count = lax.axis_size(RING)
    odd = [(i, (i + 1) % count) for i in range(1, count, 2)]
    return odd, [(there, here) for here, there in odd]


def chip_swap(shard):
    count = lax.axis_size(RING)
    return lax.ppermute(shard, RING, [(i, i ^ 1) for i in range(count)])


def body(source, send_ids, send_counts, tile_slot, tile_target, tile_weights):
    members = lax.axis_size("blk")
    capacity = send_ids.shape[1] // members
    picked = pick(members, capacity, send_ids, send_counts, source)
    later_blocks = [exchanged(picked[k - members], k) for k in range(EARLY, members)]
    early_blocks = [picked[0]] + [exchanged(picked[1 + n], 1 + n // capacity) for n in range((EARLY - 1) * capacity)]
    tiles = (tile_slot, tile_target, tile_weights)
    left_across, left_chip = spread(members, capacity, ((0, 3), (3, 0)), *tiles)
    sums, first = early(left_across, early_blocks)
    from_odd, from_even = ring_pairs()
    message_odd, later = send_edge(True, left_across, sums, *later_blocks)
    message_odd = lax.ppermute(message_odd, RING, from_odd)
    message_even = lax.ppermute(send_edge(False, left_across, sums, later)[0], RING, from_even)
    messages_chip = [chip_swap(message) for message in chip_edge(PARTS, left_chip, first, later)]
    tiles, later = lax.optimization_barrier((tiles, later))
    own_left = spread(members, capacity, ((1, 2), (2, 1)), *tiles)
    own_across, own_chip = middle(*own_left, first, later)
    out = finish(None, PARTS, own_chip, messages_chip)
    out = finish(0, WHOLE, own_across, [message_odd], out)
    out = finish(1, WHOLE, own_across, [message_even], out)
    return out.reshape(2 * ROWS, COLS)


def solution(mesh):
    spec = P(("grp", "blk"), None)
    return jax.shard_map(body, mesh=mesh, in_specs=(spec,) * 6, out_specs=spec, check_vma=False)
```

```python
import functools

import jax
import jax.numpy as jnp
from jax import lax
from jax.experimental import pallas as pl
from jax.experimental.pallas import tpu as pltpu
from jax.sharding import PartitionSpec as P

COLS = 256
BLOCK = 64
EB = 16
CHUNK = 2 * BLOCK
ROWS = EB * BLOCK
GROUP = 64
EARLY = 2
SLABS = 4
RING = ("grp", "blk")
WHOLE = (ROWS,)
PARTS = (ROWS // 2, ROWS // 2)
FLOOR = 2.0**-110
VMEM = pl.BlockSpec(memory_space=pltpu.VMEM)
SMEM = pl.BlockSpec(memory_space=pltpu.SMEM)
ANY = pl.BlockSpec(memory_space=pl.ANY)


def params():
    return pltpu.CompilerParams(vmem_limit_bytes=40 * 1024 * 1024)


def cost(flops, nbytes):
    return pl.CostEstimate(flops=flops, bytes_accessed=nbytes, transcendentals=0)


def parity():
    return lax.rem(lax.axis_index("grp") * lax.axis_size("blk") + lax.axis_index("blk"), 2)


def partner(own, k, members):
    if members & (members - 1) == 0:
        return lax.bitwise_xor(own, jnp.int32(k))
    return lax.rem(own + k, members)


def step_of(own, sender, members):
    if members & (members - 1) == 0:
        return lax.bitwise_xor(jnp.full_like(sender, own), sender)
    return lax.rem(own - sender + members, members)


def pick_kernel(members, capacity, ids, counts, source, *refs):
    picked, (blocks, id_list, count_list, sems) = list(refs[:-4]), refs[-4:]
    own = lax.axis_index("blk")
    copies = [
        pltpu.make_async_copy(here, there, sems.at[n])
        for n, (here, there) in enumerate(((ids, id_list), (counts, count_list), (source, blocks)))
    ]
    for copy in copies:
        copy.start()
    for copy in copies:
        copy.wait()
    at = 0
    for k in range(members):
        reader = partner(own, k, members)
        for j in range(capacity):
            start = pl.multiple_of(id_list[0, reader * capacity + j] * BLOCK, BLOCK)
            live = (j < count_list[0, reader]).astype(jnp.float32).astype(jnp.bfloat16)
            if at == picked[0].shape[0]:
                picked.pop(0)
                at = 0
            picked[0][at : at + BLOCK] = blocks[pl.ds(start, BLOCK)] * live
            at += BLOCK


def in_hbm(*arrays):
    return [pltpu.with_memory_space_constraint(x, pltpu.HBM) for x in arrays]


def pick(members, capacity, send_ids, send_counts, source):
    out_shape = [pltpu.VMEM((capacity * BLOCK, COLS), jnp.bfloat16)] * members
    return pl.pallas_call(
        functools.partial(pick_kernel, members, capacity),
        out_shape=out_shape,
        in_specs=[ANY] * 3,
        out_specs=[VMEM] * len(out_shape),
        scratch_shapes=[
            pltpu.VMEM(source.shape, source.dtype),
            pltpu.SMEM(send_ids.shape, jnp.int32),
            pltpu.SMEM(send_counts.shape, jnp.int32),
            pltpu.SemaphoreType.DMA((3,)),
        ],
        compiler_params=params(),
        name="pick",
    )(*in_hbm(send_ids, send_counts, source))


def lanes_of(k, members):
    if k < EARLY:
        return k * CHUNK, (EARLY + k) * CHUNK
    return (EARLY + k) * CHUNK, (members + k) * CHUNK


def spread_kernel(members, capacity, quarters, *refs):
    here, outs, (slots, targets, weights, sems) = refs[:3], refs[3:-4], refs[-4:]
    slab = weights.shape[1] // SLABS
    copies = [pltpu.make_async_copy(here[n], (slots, targets)[n], sems.at[n]) for n in range(2)]
    for n in range(SLABS):
        part = (slice(None), pl.ds(n * slab, slab))
        copies.append(pltpu.make_async_copy(here[2].at[part], weights.at[part], sems.at[2 + n]))
    for copy in copies:
        copy.start()
    for copy in copies[:2]:
        copy.wait()
    own = lax.axis_index("blk")
    tiles = weights.shape[0]
    count = len(quarters)
    slot = slots[...]
    sender = slot // capacity
    place = step_of(own, sender, members) * capacity + slot % capacity
    target = targets[...]
    rows = lax.broadcasted_iota(jnp.int32, (count * EB, tiles), 0)
    wanted = rows
    for n, (even, odd) in enumerate(quarters):
        wanted = jnp.where(rows // EB == n, rows % EB + jnp.where(parity() == 1, odd, even) * EB, wanted)
    hit = target == wanted
    table = jnp.concatenate(
        [
            jnp.concatenate(
                [(hit & (place == k * capacity + j)).astype(jnp.float32) for j in range(capacity)], axis=1
            )
            for k in range(members)
        ],
        axis=0,
    ).astype(jnp.bfloat16)
    left = (lax.broadcasted_iota(jnp.int32, (1, CHUNK), 1) < BLOCK).astype(jnp.float32)
    low = left.astype(jnp.bfloat16)
    high = (1.0 - left).astype(jnp.bfloat16)

    def step(c, _):
        x = weights[:, pl.ds(pl.multiple_of(c * CHUNK, CHUNK), CHUNK)]
        swapped = jnp.concatenate([x[:, BLOCK:], x[:, :BLOCK]], axis=1)
        right = jnp.concatenate(
            [
                jnp.concatenate([x * low, swapped * low], axis=1),
                jnp.concatenate([swapped * high, x * high], axis=1),
            ],
            axis=0,
        )
        sums = jnp.dot(table, right, preferred_element_type=jnp.float32)
        coarse = sums.astype(jnp.bfloat16)
        fine = (sums - coarse.astype(jnp.float32)).astype(jnp.bfloat16)
        for k in range(members):
            for n in range(count):
                top = (k * count + n) * EB
                for h in range(2):
                    row = pl.ds(pl.multiple_of((2 * c + h) * EB, EB), EB)
                    part = (slice(top, top + EB), slice(h * CHUNK, (h + 1) * CHUNK))
                    for lanes, value in zip(lanes_of(k, members), (coarse, fine)):
                        outs[n][row, lanes : lanes + CHUNK] = value[part]
        return 0

    each = slab // CHUNK
    for n in range(SLABS):
        copies[2 + n].wait()
        lax.fori_loop(n * each, (n + 1) * each, step, 0, unroll=each)


def spread(members, capacity, quarters, slots, targets, weights):
    shape = (ROWS, 2 * members * CHUNK)
    tiles = weights.shape[0]
    return pl.pallas_call(
        functools.partial(spread_kernel, members, capacity, quarters),
        out_shape=[pltpu.VMEM(shape, jnp.bfloat16)] * len(quarters),
        in_specs=[ANY] * 3,
        out_specs=[VMEM] * len(quarters),
        scratch_shapes=[
            pltpu.VMEM(slots.shape, jnp.int32),
            pltpu.VMEM(targets.shape, jnp.int32),
            pltpu.VMEM(weights.shape, weights.dtype),
            pltpu.SemaphoreType.DMA((2 + SLABS,)),
        ],
        compiler_params=params(),
        cost_estimate=cost(2 * members * EB * len(quarters) * 2 * tiles * 8192, 6 * 2**20),
        name="spread",
    )(*in_hbm(slots, targets, weights))


def stacked(blocks, both):
    start = 0
    for block in 2 * blocks:
        both[start : start + block.shape[0]] = block[...]
        start += block.shape[0]


def early_kernel(left, *refs):
    blocks, (sums, both) = refs[:-2], refs[-2:]
    stacked(blocks, both)
    sums[...] = jnp.dot(left[:, : both.shape[0]], both[...], preferred_element_type=jnp.float32)


def early(left, blocks):
    depth = 2 * EARLY * CHUNK
    return pl.pallas_call(
        early_kernel,
        out_shape=[pltpu.VMEM((ROWS, COLS), jnp.float32), pltpu.VMEM((depth, COLS), jnp.bfloat16)],
        in_specs=[VMEM] * (1 + len(blocks)),
        out_specs=[VMEM] * 2,
        compiler_params=params(),
        cost_estimate=cost(2 * ROWS * depth * COLS, 2 * 2**20),
        name="early",
    )(left, *blocks)


def coded(piece, message, powers):
    count = piece.shape[0]
    if count // GROUP < powers.shape[0]:
        powers[...] = jnp.zeros_like(powers)
    for g in range(count // GROUP):
        rows = piece[g * GROUP : (g + 1) * GROUP]
        most = jnp.maximum(jnp.max(jnp.abs(rows), axis=0, keepdims=True), FLOOR)
        power = jnp.floor(jnp.log2(most) + 0.001) + 1.0
        whole = jnp.round(rows * jnp.exp2(15.0 - power)).astype(jnp.int32)
        message[g * GROUP : (g + 1) * GROUP] = whole.astype(jnp.int16)
        powers[g : g + 1] = power.astype(jnp.int32)
    message[count : count + powers.shape[0]] = powers[...].astype(jnp.int16)


def product(left, first, later):
    both = jnp.concatenate([first[...], later[...]], axis=0)
    return jnp.dot(left, both, preferred_element_type=jnp.float32)


def send_kernel(odd, left, sums, *refs):
    blocks, message, refs = refs[: -3 if odd else -2], refs[-3 if odd else -2], refs[-2 if odd else -1 :]
    if odd:
        both, powers = refs
        stacked(blocks, both)
    else:
        both, powers = blocks[0], refs[0]

    @pl.when(parity() == (1 if odd else 0))
    def _():
        start = left.shape[1] - both.shape[0]
        piece = jnp.dot(left[:, start:], both[...], preferred_element_type=jnp.float32)
        coded(sums[...] + piece, message, powers)


def scales(count):
    return max(count // GROUP, 16)


def message_of(count):
    return pltpu.VMEM((count + scales(count), COLS), jnp.int16)


def powers_of(count):
    return pltpu.VMEM((scales(count), COLS), jnp.int32)


def send_edge(odd, left, sums, *blocks):
    depth = 2 * sum(block.shape[0] for block in blocks) if odd else blocks[0].shape[0]
    out_shape = [message_of(ROWS)]
    if odd:
        out_shape.append(pltpu.VMEM((depth, COLS), jnp.bfloat16))
    return pl.pallas_call(
        functools.partial(send_kernel, odd),
        out_shape=out_shape,
        in_specs=[VMEM] * (2 + len(blocks)),
        out_specs=[VMEM] * len(out_shape),
        scratch_shapes=[powers_of(ROWS)],
        compiler_params=params(),
        cost_estimate=cost(2 * ROWS * depth * COLS, 2 * 2**20),
        name="send_odd" if odd else "send_even",
    )(left, sums, *blocks)


def chip_kernel(parts, left, first, later, *refs):
    start = 0
    for count, message, powers in zip(parts, refs[: len(parts)], refs[len(parts) :]):
        coded(product(left[start : start + count], first, later), message, powers)
        start += count


def chip_edge(parts, left, first, later):
    return pl.pallas_call(
        functools.partial(chip_kernel, parts),
        out_shape=[message_of(count) for count in parts],
        in_specs=[VMEM] * 3,
        out_specs=[VMEM] * len(parts),
        scratch_shapes=[powers_of(count) for count in parts],
        compiler_params=params(),
        cost_estimate=cost(2 * ROWS * left.shape[1] * COLS, 2 * 2**20),
        name="chip",
    )(left, first, later)


def middle_kernel(left_0, left_1, first, later, *outs):
    step = 256
    for left, out in zip((left_0, left_1), outs):
        for start in range(0, ROWS, step):
            out[start : start + step] = product(left[start : start + step], first, later)


def middle(left_0, left_1, first, later):
    return pl.pallas_call(
        middle_kernel,
        out_shape=[pltpu.VMEM((ROWS, COLS), jnp.float32)] * 2,
        in_specs=[VMEM] * 4,
        out_specs=[VMEM] * 2,
        compiler_params=params(),
        cost_estimate=cost(4 * ROWS * left_0.shape[1] * COLS, 4 * 2**20),
        name="middle",
    )(left_0, left_1, first, later)


def finish_half(half, parts, own, messages, out, rows, sems):
    pitch = BLOCK + 8
    targets = rows.reshape(COLS // 128, EB, pitch, 128)
    some = EB // 2
    copies = []
    for first in range(0, EB, some):
        i = 0
        for count, message in zip(parts, messages):
            scale = jnp.exp2(message[count : count + scales(count)].astype(jnp.float32) - 15.0)
            for at in range(0, count, EB):
                g = at // GROUP
                value = message[at : at + EB].astype(jnp.float32)[first : first + some]
                value = own[i * EB + first : i * EB + first + some] + value * scale[g : g + 1]
                for n in range(COLS // 128):
                    place = pl.ds(first * pitch + i, some, stride=pitch)
                    rows[n, place] = value[:, n * 128 : (n + 1) * 128]
                i += 1
        for n in range(COLS // 128):
            here = targets.at[n, pl.ds(first, some), pl.ds(0, BLOCK)]
            there = out.at[pl.ds(half * EB + first, some), :, pl.ds(n * 128, 128)]
            copies.append(pltpu.make_async_copy(here, there, sems.at[len(copies)]))
            copies[-1].start()
    for copy in copies:
        copy.wait()


def finish_kernel(role, parts, own, *refs):
    messages, rest = refs[: len(parts)], refs[-3:]
    if role is None:
        finish_half(1 - parity(), parts, own, messages, *rest)
        return

    @pl.when(parity() == role)
    def _():
        finish_half(role, parts, own, messages, *rest)


def finish(role, parts, own, messages, out=None):
    given = [] if out is None else [out]
    return pl.pallas_call(
        functools.partial(finish_kernel, role, parts),
        out_shape=jax.ShapeDtypeStruct((2 * EB, BLOCK, COLS), jnp.float32),
        in_specs=[VMEM] * (1 + len(parts)) + [ANY] * len(given),
        out_specs=ANY,
        scratch_shapes=[
            pltpu.VMEM((COLS // 128, EB * (BLOCK + 8), 128), jnp.float32),
            pltpu.SemaphoreType.DMA((2 * COLS // 128,)),
        ],
        input_output_aliases={} if out is None else {1 + len(parts): 0},
        compiler_params=params(),
        cost_estimate=cost(3 * ROWS * COLS, 2 * 2**20),
        name="finish",
    )(own, *messages, *given)


def passed_along(shard, axis, by):
    count = lax.axis_size(axis)
    return lax.ppermute(shard, axis, [(i, (i + by) % count) for i in range(count)])


def exchanged(shard, k):
    members = lax.axis_size("blk")
    if members & (members - 1) == 0:
        return lax.ppermute(shard, "blk", [(i, i ^ k) for i in range(members)])
    return passed_along(shard, "blk", k)


def chip_swap(shard):
    count = lax.axis_size(RING)
    return lax.ppermute(shard, RING, [(i, i ^ 1) for i in range(count)])


def body(source, send_ids, send_counts, tile_slot, tile_target, tile_weights):
    members = lax.axis_size("blk")
    capacity = send_ids.shape[1] // members
    picked = pick(members, capacity, send_ids, send_counts, source)
    blocks = [picked[0]] + [exchanged(picked[k], k) for k in range(1, members)]
    early_blocks, later_blocks = blocks[:EARLY], blocks[EARLY:]
    tiles = (tile_slot, tile_target, tile_weights)
    left_across, left_chip = spread(members, capacity, ((0, 3), (3, 0)), *tiles)
    sums, first = early(left_across, early_blocks)
    message_odd, later = send_edge(True, left_across, sums, *later_blocks)
    message_odd = passed_along(message_odd, RING, 1)
    message_even = passed_along(send_edge(False, left_across, sums, later)[0], RING, -1)
    messages_chip = [chip_swap(message) for message in chip_edge(PARTS, left_chip, first, later)]
    tiles, later = lax.optimization_barrier((tiles, later))
    own_left = spread(members, capacity, ((1, 2), (2, 1)), *tiles)
    own_across, own_chip = middle(*own_left, first, later)
    out = finish(None, PARTS, own_chip, messages_chip)
    out = finish(0, WHOLE, own_across, [message_odd], out)
    out = finish(1, WHOLE, own_across, [message_even], out)
    return out.reshape(2 * ROWS, COLS)


def solution(mesh):
    spec = P(("grp", "blk"), None)
    return jax.shard_map(body, mesh=mesh, in_specs=(spec,) * 6, out_specs=spec, check_vma=False)
```

```python
import functools

import jax
import jax.numpy as jnp
from jax import lax
from jax.experimental import pallas as pl
from jax.experimental.pallas import tpu as pltpu
from jax.sharding import PartitionSpec as P

COLS = 256
BLOCK = 64
EB = 16
CHUNK = 2 * BLOCK
ROWS = EB * BLOCK
GROUP = 64
EARLY = 2
ACROSS = (ROWS,)
PARTS = (ROWS // 2, ROWS // 2)
FLOOR = 2.0**-110
VMEM = pl.BlockSpec(memory_space=pltpu.VMEM)
SMEM = pl.BlockSpec(memory_space=pltpu.SMEM)
ANY = pl.BlockSpec(memory_space=pl.ANY)


def params():
    return pltpu.CompilerParams(vmem_limit_bytes=40 * 1024 * 1024)


def cost(flops, nbytes):
    return pl.CostEstimate(flops=flops, bytes_accessed=nbytes, transcendentals=0)


def parity():
    return lax.rem(lax.axis_index("grp") * lax.axis_size("blk") + lax.axis_index("blk"), 2)


def pick_kernel(members, capacity, ids, counts, source, slots, targets, *refs):
    picked, (slot_list, target_list, blocks, id_list, count_list, sems) = refs[:members], refs[members:]
    own = lax.axis_index("blk")
    pairs = (
        (ids, id_list),
        (counts, count_list),
        (source, blocks),
        (slots, slot_list),
        (targets, target_list),
    )
    copies = [pltpu.make_async_copy(here, there, sems.at[n]) for n, (here, there) in enumerate(pairs)]
    for copy in copies:
        copy.start()
    for copy in copies[:3]:
        copy.wait()
    for k in range(members):
        reader = lax.rem(own + k, members)
        for j in range(capacity):
            start = pl.multiple_of(id_list[0, reader * capacity + j] * BLOCK, BLOCK)
            live = (j < count_list[0, reader]).astype(jnp.float32).astype(jnp.bfloat16)
            picked[k][j * BLOCK : (j + 1) * BLOCK] = blocks[pl.ds(start, BLOCK)] * live
    for copy in copies[3:]:
        copy.wait()


def in_hbm(*arrays):
    return [pltpu.with_memory_space_constraint(x, pltpu.HBM) for x in arrays]


def pick(members, capacity, send_ids, send_counts, source, slots, targets):
    shape = (capacity * BLOCK, COLS)
    results = pl.pallas_call(
        functools.partial(pick_kernel, members, capacity),
        out_shape=[pltpu.VMEM(shape, jnp.bfloat16)] * members
        + [pltpu.VMEM(slots.shape, jnp.int32), pltpu.VMEM(targets.shape, jnp.int32)],
        in_specs=[ANY] * 5,
        out_specs=[VMEM] * (members + 2),
        scratch_shapes=[
            pltpu.VMEM(source.shape, source.dtype),
            pltpu.SMEM(send_ids.shape, jnp.int32),
            pltpu.SMEM(send_counts.shape, jnp.int32),
            pltpu.SemaphoreType.DMA((5,)),
        ],
        compiler_params=params(),
        name="pick",
    )(*in_hbm(send_ids, send_counts, source, slots, targets))
    return results[:members], results[members:]


def lanes_of(k, members):
    if k < EARLY:
        return k * CHUNK, (EARLY + k) * CHUNK
    return (EARLY + k) * CHUNK, (members + k) * CHUNK


def spread_kernel(members, capacity, quarters, slots, targets, weights, *refs):
    outs, (held, sems) = refs[:-2], refs[-2:]
    half = weights.shape[1] // 2
    parts = [held.at[:, pl.ds(n * half, half)] for n in range(2)]
    copies = [pltpu.make_async_copy(weights.at[:, pl.ds(n * half, half)], parts[n], sems.at[n]) for n in range(2)]
    for copy in copies:
        copy.start()
    own = lax.axis_index("blk")
    tiles = weights.shape[0]
    count = len(quarters)
    slot = slots[...]
    sender = slot // capacity
    place = lax.rem(own - sender + members, members) * capacity + slot % capacity
    target = targets[...]
    rows = lax.broadcasted_iota(jnp.int32, (count * EB, tiles), 0)
    wanted = rows
    for n, (even, odd) in enumerate(quarters):
        wanted = jnp.where(rows // EB == n, rows % EB + jnp.where(parity() == 1, odd, even) * EB, wanted)
    hit = target == wanted
    table = jnp.concatenate(
        [
            jnp.concatenate(
                [(hit & (place == k * capacity + j)).astype(jnp.float32) for j in range(capacity)], axis=1
            )
            for k in range(members)
        ],
        axis=0,
    ).astype(jnp.bfloat16)
    left = (lax.broadcasted_iota(jnp.int32, (1, CHUNK), 1) < BLOCK).astype(jnp.float32)
    low = left.astype(jnp.bfloat16)
    high = (1.0 - left).astype(jnp.bfloat16)

    def step(part, first, c, _):
        x = part[:, pl.ds(pl.multiple_of(c * CHUNK, CHUNK), CHUNK)]
        c = c + first
        swapped = jnp.concatenate([x[:, BLOCK:], x[:, :BLOCK]], axis=1)
        right = jnp.concatenate(
            [
                jnp.concatenate([x * low, swapped * low], axis=1),
                jnp.concatenate([swapped * high, x * high], axis=1),
            ],
            axis=0,
        )
        sums = jnp.dot(table, right, preferred_element_type=jnp.float32)
        coarse = sums.astype(jnp.bfloat16)
        fine = (sums - coarse.astype(jnp.float32)).astype(jnp.bfloat16)
        for k in range(members):
            for n in range(count):
                top = (k * count + n) * EB
                for h in range(2):
                    row = pl.ds(pl.multiple_of((2 * c + h) * EB, EB), EB)
                    part = (slice(top, top + EB), slice(h * CHUNK, (h + 1) * CHUNK))
                    for lanes, value in zip(lanes_of(k, members), (coarse, fine)):
                        outs[n][row, lanes : lanes + CHUNK] = value[part]
        return 0

    each = half // CHUNK
    for n in range(2):
        copies[n].wait()
        lax.fori_loop(0, each, functools.partial(step, parts[n], n * each), 0, unroll=each)


def spread(members, capacity, quarters, slots, targets, weights):
    shape = (ROWS, 2 * members * CHUNK)
    tiles = weights.shape[0]
    return pl.pallas_call(
        functools.partial(spread_kernel, members, capacity, quarters),
        out_shape=[pltpu.VMEM(shape, jnp.bfloat16)] * len(quarters),
        in_specs=[VMEM] * 2 + [ANY],
        out_specs=[VMEM] * len(quarters),
        scratch_shapes=[
            pltpu.VMEM(weights.shape, weights.dtype),
            pltpu.SemaphoreType.DMA((2,)),
        ],
        compiler_params=params(),
        cost_estimate=cost(2 * members * EB * len(quarters) * 2 * tiles * 8192, 6 * 2**20),
        name="spread",
    )(slots, targets, *in_hbm(weights))


def stacked(blocks, both):
    rows = blocks[0].shape[0]
    for half in range(2):
        for k, block in enumerate(blocks):
            start = (half * len(blocks) + k) * rows
            both[start : start + rows] = block[...]


def early_kernel(left, *refs):
    blocks, (sums, both) = refs[:-2], refs[-2:]
    stacked(blocks, both)
    sums[...] = jnp.dot(left[:, : both.shape[0]], both[...], preferred_element_type=jnp.float32)


def early(left, blocks):
    depth = 2 * EARLY * CHUNK
    return pl.pallas_call(
        early_kernel,
        out_shape=[pltpu.VMEM((ROWS, COLS), jnp.float32), pltpu.VMEM((depth, COLS), jnp.bfloat16)],
        in_specs=[VMEM] * (1 + len(blocks)),
        out_specs=[VMEM] * 2,
        compiler_params=params(),
        cost_estimate=cost(2 * ROWS * depth * COLS, 2 * 2**20),
        name="early",
    )(left, *blocks)


def coded(piece, message, powers):
    count = piece.shape[0]
    if count // GROUP < powers.shape[0]:
        powers[...] = jnp.zeros_like(powers)
    for g in range(count // GROUP):
        rows = piece[g * GROUP : (g + 1) * GROUP]
        most = jnp.maximum(jnp.max(jnp.abs(rows), axis=0, keepdims=True), FLOOR)
        power = jnp.floor(jnp.log2(most) + 0.001) + 1.0
        whole = jnp.round(rows * jnp.exp2(15.0 - power)).astype(jnp.int32)
        message[g * GROUP : (g + 1) * GROUP] = whole.astype(jnp.int16)
        powers[g : g + 1] = power.astype(jnp.int32)
    message[count : count + powers.shape[0]] = powers[...].astype(jnp.int16)


def product(left, first, later):
    both = jnp.concatenate([first[...], later[...]], axis=0)
    return jnp.dot(left, both, preferred_element_type=jnp.float32)


def across_kernel(parts, left, sums, *refs):
    blocks, refs = refs[: -2 * len(parts) - 1], refs[-2 * len(parts) - 1 :]
    messages, both, powers = refs[: len(parts)], refs[len(parts)], refs[len(parts) + 1 :]
    stacked(blocks, both)
    start = left.shape[1] - both.shape[0]
    piece = sums[...] + jnp.dot(left[:, start:], both[...], preferred_element_type=jnp.float32)
    first = 0
    for count, message, power in zip(parts, messages, powers):
        coded(piece[first : first + count], message, power)
        first += count


def scales(count):
    return max(count // GROUP, 16)


def message_of(count):
    return pltpu.VMEM((count + scales(count), COLS), jnp.int16)


def powers_of(count):
    return pltpu.VMEM((scales(count), COLS), jnp.int32)


def across_edge(parts, left, sums, blocks):
    depth = 2 * len(blocks) * CHUNK
    return pl.pallas_call(
        functools.partial(across_kernel, parts),
        out_shape=[message_of(count) for count in parts] + [pltpu.VMEM((depth, COLS), jnp.bfloat16)],
        in_specs=[VMEM] * (2 + len(blocks)),
        out_specs=[VMEM] * (len(parts) + 1),
        scratch_shapes=[powers_of(count) for count in parts],
        compiler_params=params(),
        cost_estimate=cost(2 * ROWS * depth * COLS, 2 * 2**20),
        name="across",
    )(left, sums, *blocks)


def chip_kernel(parts, left, first, later, *refs):
    start = 0
    for count, message, powers in zip(parts, refs[: len(parts)], refs[len(parts) :]):
        coded(product(left[start : start + count], first, later), message, powers)
        start += count


def chip_edge(parts, left, first, later):
    return pl.pallas_call(
        functools.partial(chip_kernel, parts),
        out_shape=[message_of(count) for count in parts],
        in_specs=[VMEM] * 3,
        out_specs=[VMEM] * len(parts),
        scratch_shapes=[powers_of(count) for count in parts],
        compiler_params=params(),
        cost_estimate=cost(2 * ROWS * left.shape[1] * COLS, 2 * 2**20),
        name="chip",
    )(left, first, later)


def middle_kernel(left_0, left_1, first, later, *outs):
    step = 256
    for left, out in zip((left_0, left_1), outs):
        for start in range(0, ROWS, step):
            out[start : start + step] = product(left[start : start + step], first, later)


def middle(left_0, left_1, first, later):
    return pl.pallas_call(
        middle_kernel,
        out_shape=[pltpu.VMEM((ROWS, COLS), jnp.float32)] * 2,
        in_specs=[VMEM] * 4,
        out_specs=[VMEM] * 2,
        compiler_params=params(),
        cost_estimate=cost(4 * ROWS * left_0.shape[1] * COLS, 4 * 2**20),
        name="middle",
    )(left_0, left_1, first, later)


def finish_kernel(across, low, parts, own, *refs):
    messages, (out, rows, sems) = refs[: len(parts)], refs[-3:]
    half = parity() if across else 1 - parity()
    high = low + sum(parts) // EB
    pitch = high - low + 8
    targets = rows.reshape(COLS // 128, EB, pitch, 128)
    some = EB // 2
    copies = []
    for first in range(0, EB, some):
        i = low
        for count, message in zip(parts, messages):
            scale = jnp.exp2(message[count : count + scales(count)].astype(jnp.float32) - 15.0)
            for at in range(0, count, EB):
                g = at // GROUP
                value = message[at : at + EB].astype(jnp.float32)[first : first + some]
                value = own[i * EB + first : i * EB + first + some] + value * scale[g : g + 1]
                for n in range(COLS // 128):
                    place = pl.ds(first * pitch + i - low, some, stride=pitch)
                    rows[n, place] = value[:, n * 128 : (n + 1) * 128]
                i += 1
        for n in range(COLS // 128):
            here = targets.at[n, pl.ds(first, some), pl.ds(0, high - low)]
            there = out.at[pl.ds(half * EB + first, some), pl.ds(low, high - low), pl.ds(n * 128, 128)]
            copies.append(pltpu.make_async_copy(here, there, sems.at[len(copies)]))
            copies[-1].start()
    for copy in copies:
        copy.wait()


def finish(across, low, parts, own, messages, out=None):
    given = [] if out is None else [out]
    pitch = sum(parts) // EB + 8
    return pl.pallas_call(
        functools.partial(finish_kernel, across, low, parts),
        out_shape=jax.ShapeDtypeStruct((2 * EB, BLOCK, COLS), jnp.float32),
        in_specs=[VMEM] * (1 + len(parts)) + [ANY] * len(given),
        out_specs=ANY,
        scratch_shapes=[
            pltpu.VMEM((COLS // 128, EB * pitch, 128), jnp.float32),
            pltpu.SemaphoreType.DMA((2 * COLS // 128,)),
        ],
        input_output_aliases={} if out is None else {1 + len(parts): 0},
        compiler_params=params(),
        cost_estimate=cost(3 * sum(parts) * COLS, 2 * 2**20 * sum(parts) // ROWS),
        name="finish",
    )(own, *messages, *given)


def passed_along(shard, axis, by):
    count = lax.axis_size(axis)
    return lax.ppermute(shard, axis, [(i, (i + by) % count) for i in range(count)])


def ring_swap(shard, across):
    axes = ("grp", "blk")
    count = lax.axis_size(axes)
    if across:
        return lax.ppermute(shard, axes, [(i, (i + (1 if i % 2 else -1)) % count) for i in range(count)])
    return lax.ppermute(shard, axes, [(i, i ^ 1) for i in range(count)])


def body(source, send_ids, send_counts, tile_slot, tile_target, tile_weights):
    members = lax.axis_size("blk")
    capacity = send_ids.shape[1] // members
    picked, tiles = pick(
        members, capacity, send_ids, send_counts, source, tile_slot, tile_target
    )
    blocks = [picked[0]] + [passed_along(picked[k], "blk", k) for k in range(1, members)]
    (left_across,) = spread(members, capacity, ((0, 3),), *tiles, tile_weights)
    sums, first = early(left_across, blocks[:EARLY])
    message_across, later = across_edge(ACROSS, left_across, sums, blocks[EARLY:])
    message_across = ring_swap(message_across, True)
    tiles, later = lax.optimization_barrier((tiles, later))
    left_chip, *own_left = spread(members, capacity, ((3, 0), (1, 2), (2, 1)), *tiles, tile_weights)
    messages_chip = [ring_swap(message, False) for message in chip_edge(PARTS, left_chip, first, later)]
    own_across, own_chip = middle(*own_left, first, later)
    out = finish(False, 0, PARTS, own_chip, messages_chip)
    out = finish(True, 0, ACROSS, own_across, [message_across], out)
    return out.reshape(2 * ROWS, COLS)


def solution(mesh):
    spec = P(("grp", "blk"), None)
    return jax.shard_map(body, mesh=mesh, in_specs=(spec,) * 6, out_specs=spec, check_vma=False)
```

```python
import functools

import jax
import jax.numpy as jnp
from jax import lax
from jax.experimental import pallas as pl
from jax.experimental.pallas import tpu as pltpu
from jax.sharding import PartitionSpec as P

COLS = 256
BLOCK = 64
EB = 16
CHUNK = 2 * BLOCK
ROWS = EB * BLOCK
GROUP = 64
EARLY = 2
ACROSS = (ROWS,)
PARTS = (ROWS // 2, ROWS // 2)
FLOOR = 2.0**-110
VMEM = pl.BlockSpec(memory_space=pltpu.VMEM)
SMEM = pl.BlockSpec(memory_space=pltpu.SMEM)
ANY = pl.BlockSpec(memory_space=pl.ANY)


def params():
    return pltpu.CompilerParams(vmem_limit_bytes=40 * 1024 * 1024)


def cost(flops, nbytes):
    return pl.CostEstimate(flops=flops, bytes_accessed=nbytes, transcendentals=0)


def parity():
    return lax.rem(lax.axis_index("grp") * lax.axis_size("blk") + lax.axis_index("blk"), 2)


def pick_kernel(members, capacity, ids, counts, source, slots, targets, *refs):
    picked, (slot_list, target_list, blocks, id_list, count_list, sems) = refs[:members], refs[members:]
    own = lax.axis_index("blk")
    pairs = (
        (ids, id_list),
        (counts, count_list),
        (source, blocks),
        (slots, slot_list),
        (targets, target_list),
    )
    copies = [pltpu.make_async_copy(here, there, sems.at[n]) for n, (here, there) in enumerate(pairs)]
    for copy in copies:
        copy.start()
    for copy in copies[:3]:
        copy.wait()
    for k in range(members):
        reader = lax.rem(own + k, members)
        for j in range(capacity):
            start = pl.multiple_of(id_list[0, reader * capacity + j] * BLOCK, BLOCK)
            live = (j < count_list[0, reader]).astype(jnp.float32).astype(jnp.bfloat16)
            picked[k][j * BLOCK : (j + 1) * BLOCK] = blocks[pl.ds(start, BLOCK)] * live
    for copy in copies[3:]:
        copy.wait()


def in_hbm(*arrays):
    return [pltpu.with_memory_space_constraint(x, pltpu.HBM) for x in arrays]


def pick(members, capacity, send_ids, send_counts, source, slots, targets):
    shape = (capacity * BLOCK, COLS)
    results = pl.pallas_call(
        functools.partial(pick_kernel, members, capacity),
        out_shape=[pltpu.VMEM(shape, jnp.bfloat16)] * members
        + [pltpu.VMEM(slots.shape, jnp.int32), pltpu.VMEM(targets.shape, jnp.int32)],
        in_specs=[ANY] * 5,
        out_specs=[VMEM] * (members + 2),
        scratch_shapes=[
            pltpu.VMEM(source.shape, source.dtype),
            pltpu.SMEM(send_ids.shape, jnp.int32),
            pltpu.SMEM(send_counts.shape, jnp.int32),
            pltpu.SemaphoreType.DMA((5,)),
        ],
        compiler_params=params(),
        name="pick",
    )(*in_hbm(send_ids, send_counts, source, slots, targets))
    return results[:members], results[members:]


def lanes_of(k, members):
    if k < EARLY:
        return k * CHUNK, (EARLY + k) * CHUNK
    return (EARLY + k) * CHUNK, (members + k) * CHUNK


def spread_kernel(members, capacity, quarters, slots, targets, weights, *refs):
    outs, (held, sems) = refs[:-2], refs[-2:]
    half = weights.shape[1] // 2
    parts = [held.at[:, pl.ds(n * half, half)] for n in range(2)]
    copies = [pltpu.make_async_copy(weights.at[:, pl.ds(n * half, half)], parts[n], sems.at[n]) for n in range(2)]
    for copy in copies:
        copy.start()
    own = lax.axis_index("blk")
    tiles = weights.shape[0]
    count = len(quarters)
    slot = slots[...]
    sender = slot // capacity
    place = lax.rem(own - sender + members, members) * capacity + slot % capacity
    target = targets[...]
    rows = lax.broadcasted_iota(jnp.int32, (count * EB, tiles), 0)
    wanted = rows
    for n, (even, odd) in enumerate(quarters):
        wanted = jnp.where(rows // EB == n, rows % EB + jnp.where(parity() == 1, odd, even) * EB, wanted)
    hit = target == wanted
    table = jnp.concatenate(
        [
            (hit & (place == k * capacity + j)).astype(jnp.float32)
            for j in range(capacity)
            for k in range(members)
        ],
        axis=0,
    ).astype(jnp.bfloat16)
    side = members * count * EB
    left = lax.broadcasted_iota(jnp.int32, (side, CHUNK), 1) < BLOCK

    def step(part, first, c, _):
        x = part[:, pl.ds(pl.multiple_of(c * CHUNK, CHUNK), CHUNK)]
        c = c + first
        sums = jnp.dot(table, x, preferred_element_type=jnp.float32)
        one, two = sums[:side], sums[side:]
        halves = (
            jnp.where(left, one, pltpu.roll(two, BLOCK, 1)),
            jnp.where(left, pltpu.roll(one, BLOCK, 1), two),
        )
        for h, value in enumerate(halves):
            coarse = value.astype(jnp.bfloat16)
            fine = (value - coarse.astype(jnp.float32)).astype(jnp.bfloat16)
            row = pl.ds(pl.multiple_of((2 * c + h) * EB, EB), EB)
            for k in range(members):
                for n in range(count):
                    top = (k * count + n) * EB
                    for lanes, part in zip(lanes_of(k, members), (coarse, fine)):
                        outs[n][row, lanes : lanes + CHUNK] = part[top : top + EB]
        return 0

    each = half // CHUNK
    for n in range(2):
        copies[n].wait()
        lax.fori_loop(0, each, functools.partial(step, parts[n], n * each), 0, unroll=each)


def spread(members, capacity, quarters, slots, targets, weights):
    shape = (ROWS, 2 * members * CHUNK)
    tiles = weights.shape[0]
    return pl.pallas_call(
        functools.partial(spread_kernel, members, capacity, quarters),
        out_shape=[pltpu.VMEM(shape, jnp.bfloat16)] * len(quarters),
        in_specs=[VMEM] * 2 + [ANY],
        out_specs=[VMEM] * len(quarters),
        scratch_shapes=[
            pltpu.VMEM(weights.shape, weights.dtype),
            pltpu.SemaphoreType.DMA((2,)),
        ],
        compiler_params=params(),
        cost_estimate=cost(2 * members * EB * len(quarters) * 2 * tiles * 8192, 6 * 2**20),
        name="spread",
    )(slots, targets, *in_hbm(weights))


def stacked(blocks, both):
    rows = blocks[0].shape[0]
    for half in range(2):
        for k, block in enumerate(blocks):
            start = (half * len(blocks) + k) * rows
            both[start : start + rows] = block[...]


def early_kernel(left, *refs):
    blocks, (sums, both) = refs[:-2], refs[-2:]
    stacked(blocks, both)
    sums[...] = jnp.dot(left[:, : both.shape[0]], both[...], preferred_element_type=jnp.float32)


def early(left, blocks):
    depth = 2 * EARLY * CHUNK
    return pl.pallas_call(
        early_kernel,
        out_shape=[pltpu.VMEM((ROWS, COLS), jnp.float32), pltpu.VMEM((depth, COLS), jnp.bfloat16)],
        in_specs=[VMEM] * (1 + len(blocks)),
        out_specs=[VMEM] * 2,
        compiler_params=params(),
        cost_estimate=cost(2 * ROWS * depth * COLS, 2 * 2**20),
        name="early",
    )(left, *blocks)


def coded(piece, message, powers):
    count = piece.shape[0]
    if count // GROUP < powers.shape[0]:
        powers[...] = jnp.zeros_like(powers)
    for g in range(count // GROUP):
        rows = piece[g * GROUP : (g + 1) * GROUP]
        most = jnp.maximum(jnp.max(jnp.abs(rows), axis=0, keepdims=True), FLOOR)
        power = jnp.floor(jnp.log2(most) + 0.001) + 1.0
        whole = jnp.round(rows * jnp.exp2(15.0 - power)).astype(jnp.int32)
        message[g * GROUP : (g + 1) * GROUP] = whole.astype(jnp.int16)
        powers[g : g + 1] = power.astype(jnp.int32)
    message[count : count + powers.shape[0]] = powers[...].astype(jnp.int16)


def product(left, first, later):
    both = jnp.concatenate([first[...], later[...]], axis=0)
    return jnp.dot(left, both, preferred_element_type=jnp.float32)


def across_kernel(parts, left, sums, *refs):
    blocks, refs = refs[: -2 * len(parts) - 1], refs[-2 * len(parts) - 1 :]
    messages, both, powers = refs[: len(parts)], refs[len(parts)], refs[len(parts) + 1 :]
    stacked(blocks, both)
    start = left.shape[1] - both.shape[0]
    piece = sums[...] + jnp.dot(left[:, start:], both[...], preferred_element_type=jnp.float32)
    first = 0
    for count, message, power in zip(parts, messages, powers):
        coded(piece[first : first + count], message, power)
        first += count


def scales(count):
    return max(count // GROUP, 16)


def message_of(count):
    return pltpu.VMEM((count + scales(count), COLS), jnp.int16)


def powers_of(count):
    return pltpu.VMEM((scales(count), COLS), jnp.int32)


def across_edge(parts, left, sums, blocks):
    depth = 2 * len(blocks) * CHUNK
    return pl.pallas_call(
        functools.partial(across_kernel, parts),
        out_shape=[message_of(count) for count in parts] + [pltpu.VMEM((depth, COLS), jnp.bfloat16)],
        in_specs=[VMEM] * (2 + len(blocks)),
        out_specs=[VMEM] * (len(parts) + 1),
        scratch_shapes=[powers_of(count) for count in parts],
        compiler_params=params(),
        cost_estimate=cost(2 * ROWS * depth * COLS, 2 * 2**20),
        name="across",
    )(left, sums, *blocks)


def chip_kernel(parts, left, first, later, *refs):
    start = 0
    for count, message, powers in zip(parts, refs[: len(parts)], refs[len(parts) :]):
        coded(product(left[start : start + count], first, later), message, powers)
        start += count


def chip_edge(parts, left, first, later):
    return pl.pallas_call(
        functools.partial(chip_kernel, parts),
        out_shape=[message_of(count) for count in parts],
        in_specs=[VMEM] * 3,
        out_specs=[VMEM] * len(parts),
        scratch_shapes=[powers_of(count) for count in parts],
        compiler_params=params(),
        cost_estimate=cost(2 * ROWS * left.shape[1] * COLS, 2 * 2**20),
        name="chip",
    )(left, first, later)


def middle_kernel(left_0, left_1, first, later, *outs):
    step = 256
    for left, out in zip((left_0, left_1), outs):
        for start in range(0, ROWS, step):
            out[start : start + step] = product(left[start : start + step], first, later)


def middle(left_0, left_1, first, later):
    return pl.pallas_call(
        middle_kernel,
        out_shape=[pltpu.VMEM((ROWS, COLS), jnp.float32)] * 2,
        in_specs=[VMEM] * 4,
        out_specs=[VMEM] * 2,
        compiler_params=params(),
        cost_estimate=cost(4 * ROWS * left_0.shape[1] * COLS, 4 * 2**20),
        name="middle",
    )(left_0, left_1, first, later)


def finish_kernel(across, low, parts, own, *refs):
    messages, (out, rows, sems) = refs[: len(parts)], refs[-3:]
    half = parity() if across else 1 - parity()
    high = low + sum(parts) // EB
    pitch = high - low + 8
    targets = rows.reshape(COLS // 128, EB, pitch, 128)
    some = EB // 2
    copies = []
    for first in range(0, EB, some):
        i = low
        for count, message in zip(parts, messages):
            scale = jnp.exp2(message[count : count + scales(count)].astype(jnp.float32) - 15.0)
            for at in range(0, count, EB):
                g = at // GROUP
                value = message[at : at + EB].astype(jnp.float32)[first : first + some]
                value = own[i * EB + first : i * EB + first + some] + value * scale[g : g + 1]
                for n in range(COLS // 128):
                    place = pl.ds(first * pitch + i - low, some, stride=pitch)
                    rows[n, place] = value[:, n * 128 : (n + 1) * 128]
                i += 1
        for n in range(COLS // 128):
            here = targets.at[n, pl.ds(first, some), pl.ds(0, high - low)]
            there = out.at[pl.ds(half * EB + first, some), pl.ds(low, high - low), pl.ds(n * 128, 128)]
            copies.append(pltpu.make_async_copy(here, there, sems.at[len(copies)]))
            copies[-1].start()
    for copy in copies:
        copy.wait()


def finish(across, low, parts, own, messages, out=None):
    given = [] if out is None else [out]
    pitch = sum(parts) // EB + 8
    return pl.pallas_call(
        functools.partial(finish_kernel, across, low, parts),
        out_shape=jax.ShapeDtypeStruct((2 * EB, BLOCK, COLS), jnp.float32),
        in_specs=[VMEM] * (1 + len(parts)) + [ANY] * len(given),
        out_specs=ANY,
        scratch_shapes=[
            pltpu.VMEM((COLS // 128, EB * pitch, 128), jnp.float32),
            pltpu.SemaphoreType.DMA((2 * COLS // 128,)),
        ],
        input_output_aliases={} if out is None else {1 + len(parts): 0},
        compiler_params=params(),
        cost_estimate=cost(3 * sum(parts) * COLS, 2 * 2**20 * sum(parts) // ROWS),
        name="finish",
    )(own, *messages, *given)


def passed_along(shard, axis, by):
    count = lax.axis_size(axis)
    return lax.ppermute(shard, axis, [(i, (i + by) % count) for i in range(count)])


def ring_swap(shard, across):
    axes = ("grp", "blk")
    count = lax.axis_size(axes)
    if across:
        return lax.ppermute(shard, axes, [(i, (i + (1 if i % 2 else -1)) % count) for i in range(count)])
    return lax.ppermute(shard, axes, [(i, i ^ 1) for i in range(count)])


def body(source, send_ids, send_counts, tile_slot, tile_target, tile_weights):
    members = lax.axis_size("blk")
    capacity = send_ids.shape[1] // members
    picked, tiles = pick(
        members, capacity, send_ids, send_counts, source, tile_slot, tile_target
    )
    blocks = [picked[0]] + [passed_along(picked[k], "blk", k) for k in range(1, members)]
    (left_across,) = spread(members, capacity, ((0, 3),), *tiles, tile_weights)
    sums, first = early(left_across, blocks[:EARLY])
    message_across, later = across_edge(ACROSS, left_across, sums, blocks[EARLY:])
    message_across = ring_swap(message_across, True)
    tiles, later = lax.optimization_barrier((tiles, later))
    left_chip, *own_left = spread(members, capacity, ((3, 0), (1, 2), (2, 1)), *tiles, tile_weights)
    messages_chip = [ring_swap(message, False) for message in chip_edge(PARTS, left_chip, first, later)]
    own_across, own_chip = middle(*own_left, first, later)
    out = finish(False, 0, PARTS, own_chip, messages_chip)
    out = finish(True, 0, ACROSS, own_across, [message_across], out)
    return out.reshape(2 * ROWS, COLS)


def solution(mesh):
    spec = P(("grp", "blk"), None)
    return jax.shard_map(body, mesh=mesh, in_specs=(spec,) * 6, out_specs=spec, check_vma=False)
```

```python
import functools

import jax
import jax.numpy as jnp
from jax import lax
from jax.experimental import pallas as pl
from jax.experimental.pallas import tpu as pltpu
from jax.sharding import PartitionSpec as P

COLS = 256
BLOCK = 64
EB = 16
CHUNK = 2 * BLOCK
ROWS = EB * BLOCK
GROUP = 64
EARLY = 2
ACROSS = (ROWS,)
PARTS = (ROWS // 2, ROWS // 2)
FLOOR = 2.0**-110
VMEM = pl.BlockSpec(memory_space=pltpu.VMEM)
SMEM = pl.BlockSpec(memory_space=pltpu.SMEM)
ANY = pl.BlockSpec(memory_space=pl.ANY)


def params():
    return pltpu.CompilerParams(vmem_limit_bytes=40 * 1024 * 1024)


def cost(flops, nbytes):
    return pl.CostEstimate(flops=flops, bytes_accessed=nbytes, transcendentals=0)


def parity():
    return lax.rem(lax.axis_index("grp") * lax.axis_size("blk") + lax.axis_index("blk"), 2)


def pick_kernel(members, capacity, ids, counts, source, *refs):
    picked, (blocks, id_list, count_list, sems) = refs[:members], refs[members:]
    own = lax.axis_index("blk")
    rows = blocks.shape[0] // 2
    parts = [pl.ds(n * rows, rows) for n in range(2)]
    pairs = [(ids, id_list), (counts, count_list)] + [(source.at[part], blocks.at[part]) for part in parts]
    copies = [pltpu.make_async_copy(here, there, sems.at[n]) for n, (here, there) in enumerate(pairs)]
    for n, copy in enumerate(copies):
        copy.start(priority=n % 2)
    for copy in copies:
        copy.wait()
    for k in range(members):
        reader = lax.rem(own + k, members)
        for j in range(capacity):
            start = pl.multiple_of(id_list[0, reader * capacity + j] * BLOCK, BLOCK)
            live = (j < count_list[0, reader]).astype(jnp.float32).astype(jnp.bfloat16)
            picked[k][j * BLOCK : (j + 1) * BLOCK] = blocks[pl.ds(start, BLOCK)] * live


def in_hbm(*arrays):
    return [pltpu.with_memory_space_constraint(x, pltpu.HBM) for x in arrays]


def pick(members, capacity, send_ids, send_counts, source):
    shape = (capacity * BLOCK, COLS)
    return pl.pallas_call(
        functools.partial(pick_kernel, members, capacity),
        out_shape=[pltpu.VMEM(shape, jnp.bfloat16)] * members,
        in_specs=[ANY] * 3,
        out_specs=[VMEM] * members,
        scratch_shapes=[
            pltpu.VMEM(source.shape, source.dtype),
            pltpu.SMEM(send_ids.shape, jnp.int32),
            pltpu.SMEM(send_counts.shape, jnp.int32),
            pltpu.SemaphoreType.DMA((4,)),
        ],
        compiler_params=params(),
        name="pick",
    )(*in_hbm(send_ids, send_counts, source))


def lanes_of(k, members):
    if k < EARLY:
        return k * CHUNK, (EARLY + k) * CHUNK
    return (EARLY + k) * CHUNK, (members + k) * CHUNK


def spread_kernel(members, capacity, quarters, slots_here, targets_here, weights, *refs):
    outs, (slots, targets, held, sems) = refs[:-4], refs[-4:]
    half = weights.shape[1] // 2
    parts = [held.at[:, pl.ds(n * half, half)] for n in range(2)]
    copies = [pltpu.make_async_copy(weights.at[:, pl.ds(n * half, half)], parts[n], sems.at[n]) for n in range(2)]
    lists = ((slots_here, slots), (targets_here, targets))
    lists = [pltpu.make_async_copy(here, there, sems.at[2 + n]) for n, (here, there) in enumerate(lists)]
    for copy in lists + copies:
        copy.start()
    for copy in lists:
        copy.wait()
    own = lax.axis_index("blk")
    tiles = weights.shape[0]
    count = len(quarters)
    slot = slots[...]
    sender = slot // capacity
    place = lax.rem(own - sender + members, members) * capacity + slot % capacity
    target = targets[...]
    rows = lax.broadcasted_iota(jnp.int32, (count * EB, tiles), 0)
    wanted = rows
    for n, (even, odd) in enumerate(quarters):
        wanted = jnp.where(rows // EB == n, rows % EB + jnp.where(parity() == 1, odd, even) * EB, wanted)
    hit = target == wanted
    table = jnp.concatenate(
        [
            (hit & (place == k * capacity + j)).astype(jnp.float32)
            for j in range(capacity)
            for k in range(members)
        ],
        axis=0,
    ).astype(jnp.bfloat16)
    side = members * count * EB
    left = lax.broadcasted_iota(jnp.int32, (side, CHUNK), 1) < BLOCK

    def step(part, first, c, _):
        x = part[:, pl.ds(pl.multiple_of(c * CHUNK, CHUNK), CHUNK)]
        c = c + first
        sums = jnp.dot(table, x, preferred_element_type=jnp.float32)
        one, two = sums[:side], sums[side:]
        halves = (
            jnp.where(left, one, pltpu.roll(two, BLOCK, 1)),
            jnp.where(left, pltpu.roll(one, BLOCK, 1), two),
        )
        for h, value in enumerate(halves):
            coarse = value.astype(jnp.bfloat16)
            fine = (value - coarse.astype(jnp.float32)).astype(jnp.bfloat16)
            row = pl.ds(pl.multiple_of((2 * c + h) * EB, EB), EB)
            for k in range(members):
                for n in range(count):
                    top = (k * count + n) * EB
                    for lanes, part in zip(lanes_of(k, members), (coarse, fine)):
                        outs[n][row, lanes : lanes + CHUNK] = part[top : top + EB]
        return 0

    each = half // CHUNK
    for n in range(2):
        copies[n].wait()
        lax.fori_loop(0, each, functools.partial(step, parts[n], n * each), 0, unroll=each)


def spread(members, capacity, quarters, slots, targets, weights):
    shape = (ROWS, 2 * members * CHUNK)
    tiles = weights.shape[0]
    return pl.pallas_call(
        functools.partial(spread_kernel, members, capacity, quarters),
        out_shape=[pltpu.VMEM(shape, jnp.bfloat16)] * len(quarters),
        in_specs=[ANY] * 3,
        out_specs=[VMEM] * len(quarters),
        scratch_shapes=[
            pltpu.VMEM(slots.shape, jnp.int32),
            pltpu.VMEM(targets.shape, jnp.int32),
            pltpu.VMEM(weights.shape, weights.dtype),
            pltpu.SemaphoreType.DMA((4,)),
        ],
        compiler_params=params(),
        cost_estimate=cost(2 * members * EB * len(quarters) * 2 * tiles * 8192, 6 * 2**20),
        name="spread",
    )(*in_hbm(slots, targets, weights))


def stacked(blocks, both):
    rows = blocks[0].shape[0]
    for half in range(2):
        for k, block in enumerate(blocks):
            start = (half * len(blocks) + k) * rows
            both[start : start + rows] = block[...]


def early_kernel(left, *refs):
    blocks, (sums, both) = refs[:-2], refs[-2:]
    stacked(blocks, both)
    sums[...] = jnp.dot(left[:, : both.shape[0]], both[...], preferred_element_type=jnp.float32)


def early(left, blocks):
    depth = 2 * EARLY * CHUNK
    return pl.pallas_call(
        early_kernel,
        out_shape=[pltpu.VMEM((ROWS, COLS), jnp.float32), pltpu.VMEM((depth, COLS), jnp.bfloat16)],
        in_specs=[VMEM] * (1 + len(blocks)),
        out_specs=[VMEM] * 2,
        compiler_params=params(),
        cost_estimate=cost(2 * ROWS * depth * COLS, 2 * 2**20),
        name="early",
    )(left, *blocks)


def coded(piece, message, powers):
    count = piece.shape[0]
    if count // GROUP < powers.shape[0]:
        powers[...] = jnp.zeros_like(powers)
    for g in range(count // GROUP):
        rows = piece[g * GROUP : (g + 1) * GROUP]
        most = jnp.maximum(jnp.max(jnp.abs(rows), axis=0, keepdims=True), FLOOR)
        power = jnp.floor(jnp.log2(most) + 0.001) + 1.0
        whole = jnp.round(rows * jnp.exp2(15.0 - power)).astype(jnp.int32)
        message[g * GROUP : (g + 1) * GROUP] = whole.astype(jnp.int16)
        powers[g : g + 1] = power.astype(jnp.int32)
    message[count : count + powers.shape[0]] = powers[...].astype(jnp.int16)


def product(left, first, later):
    both = jnp.concatenate([first[...], later[...]], axis=0)
    return jnp.dot(left, both, preferred_element_type=jnp.float32)


def across_kernel(parts, left, sums, *refs):
    blocks, refs = refs[: -2 * len(parts) - 1], refs[-2 * len(parts) - 1 :]
    messages, both, powers = refs[: len(parts)], refs[len(parts)], refs[len(parts) + 1 :]
    stacked(blocks, both)
    start = left.shape[1] - both.shape[0]
    piece = sums[...] + jnp.dot(left[:, start:], both[...], preferred_element_type=jnp.float32)
    first = 0
    for count, message, power in zip(parts, messages, powers):
        coded(piece[first : first + count], message, power)
        first += count


def scales(count):
    return max(count // GROUP, 16)


def message_of(count):
    return pltpu.VMEM((count + scales(count), COLS), jnp.int16)


def powers_of(count):
    return pltpu.VMEM((scales(count), COLS), jnp.int32)


def across_edge(parts, left, sums, blocks):
    depth = 2 * len(blocks) * CHUNK
    return pl.pallas_call(
        functools.partial(across_kernel, parts),
        out_shape=[message_of(count) for count in parts] + [pltpu.VMEM((depth, COLS), jnp.bfloat16)],
        in_specs=[VMEM] * (2 + len(blocks)),
        out_specs=[VMEM] * (len(parts) + 1),
        scratch_shapes=[powers_of(count) for count in parts],
        compiler_params=params(),
        cost_estimate=cost(2 * ROWS * depth * COLS, 2 * 2**20),
        name="across",
    )(left, sums, *blocks)


def chip_kernel(parts, left, first, later, *refs):
    start = 0
    for count, message, powers in zip(parts, refs[: len(parts)], refs[len(parts) :]):
        coded(product(left[start : start + count], first, later), message, powers)
        start += count


def chip_edge(parts, left, first, later):
    return pl.pallas_call(
        functools.partial(chip_kernel, parts),
        out_shape=[message_of(count) for count in parts],
        in_specs=[VMEM] * 3,
        out_specs=[VMEM] * len(parts),
        scratch_shapes=[powers_of(count) for count in parts],
        compiler_params=params(),
        cost_estimate=cost(2 * ROWS * left.shape[1] * COLS, 2 * 2**20),
        name="chip",
    )(left, first, later)


def middle_kernel(left_0, left_1, first, later, *outs):
    step = 256
    for left, out in zip((left_0, left_1), outs):
        for start in range(0, ROWS, step):
            out[start : start + step] = product(left[start : start + step], first, later)


def middle(left_0, left_1, first, later):
    return pl.pallas_call(
        middle_kernel,
        out_shape=[pltpu.VMEM((ROWS, COLS), jnp.float32)] * 2,
        in_specs=[VMEM] * 4,
        out_specs=[VMEM] * 2,
        compiler_params=params(),
        cost_estimate=cost(4 * ROWS * left_0.shape[1] * COLS, 4 * 2**20),
        name="middle",
    )(left_0, left_1, first, later)


def finish_kernel(across, low, parts, own, *refs):
    messages, (out, rows, sems) = refs[: len(parts)], refs[-3:]
    half = parity() if across else 1 - parity()
    high = low + sum(parts) // EB
    pitch = high - low + 8
    targets = rows.reshape(COLS // 128, EB, pitch, 128)
    some = EB // 2
    copies = []
    for first in range(0, EB, some):
        i = low
        for count, message in zip(parts, messages):
            scale = jnp.exp2(message[count : count + scales(count)].astype(jnp.float32) - 15.0)
            for at in range(0, count, EB):
                g = at // GROUP
                value = message[at : at + EB].astype(jnp.float32)[first : first + some]
                value = own[i * EB + first : i * EB + first + some] + value * scale[g : g + 1]
                for n in range(COLS // 128):
                    place = pl.ds(first * pitch + i - low, some, stride=pitch)
                    rows[n, place] = value[:, n * 128 : (n + 1) * 128]
                i += 1
        for n in range(COLS // 128):
            here = targets.at[n, pl.ds(first, some), pl.ds(0, high - low)]
            there = out.at[pl.ds(half * EB + first, some), pl.ds(low, high - low), pl.ds(n * 128, 128)]
            copies.append(pltpu.make_async_copy(here, there, sems.at[len(copies)]))
            copies[-1].start()
    for copy in copies:
        copy.wait()


def finish(across, low, parts, own, messages, out=None):
    given = [] if out is None else [out]
    pitch = sum(parts) // EB + 8
    return pl.pallas_call(
        functools.partial(finish_kernel, across, low, parts),
        out_shape=jax.ShapeDtypeStruct((2 * EB, BLOCK, COLS), jnp.float32),
        in_specs=[VMEM] * (1 + len(parts)) + [ANY] * len(given),
        out_specs=ANY,
        scratch_shapes=[
            pltpu.VMEM((COLS // 128, EB * pitch, 128), jnp.float32),
            pltpu.SemaphoreType.DMA((2 * COLS // 128,)),
        ],
        input_output_aliases={} if out is None else {1 + len(parts): 0},
        compiler_params=params(),
        cost_estimate=cost(3 * sum(parts) * COLS, 2 * 2**20 * sum(parts) // ROWS),
        name="finish",
    )(own, *messages, *given)


def passed_along(shard, axis, by):
    count = lax.axis_size(axis)
    return lax.ppermute(shard, axis, [(i, (i + by) % count) for i in range(count)])


def ring_swap(shard, across):
    axes = ("grp", "blk")
    count = lax.axis_size(axes)
    if across:
        return lax.ppermute(shard, axes, [(i, (i + (1 if i % 2 else -1)) % count) for i in range(count)])
    return lax.ppermute(shard, axes, [(i, i ^ 1) for i in range(count)])


def body(source, send_ids, send_counts, tile_slot, tile_target, tile_weights):
    members = lax.axis_size("blk")
    capacity = send_ids.shape[1] // members
    picked = pick(members, capacity, send_ids, send_counts, source)
    tiles = (tile_slot, tile_target)
    blocks = [picked[0]] + [passed_along(picked[k], "blk", k) for k in range(1, members)]
    (left_across,) = spread(members, capacity, ((0, 3),), *tiles, tile_weights)
    sums, first = early(left_across, blocks[:EARLY])
    message_across, later = across_edge(ACROSS, left_across, sums, blocks[EARLY:])
    message_across = ring_swap(message_across, True)
    tiles, later = lax.optimization_barrier((tiles, later))
    left_chip, *own_left = spread(members, capacity, ((3, 0), (1, 2), (2, 1)), *tiles, tile_weights)
    messages_chip = [ring_swap(message, False) for message in chip_edge(PARTS, left_chip, first, later)]
    own_across, own_chip = middle(*own_left, first, later)
    out = finish(False, 0, PARTS, own_chip, messages_chip)
    out = finish(True, 0, ACROSS, own_across, [message_across], out)
    return out.reshape(2 * ROWS, COLS)


def solution(mesh):
    spec = P(("grp", "blk"), None)
    return jax.shard_map(body, mesh=mesh, in_specs=(spec,) * 6, out_specs=spec, check_vma=False)
```

```python
import functools

import jax
import jax.numpy as jnp
from jax import lax
from jax.experimental import pallas as pl
from jax.experimental.pallas import tpu as pltpu
from jax.sharding import PartitionSpec as P

COLS = 256
BLOCK = 64
EB = 16
CHUNK = 2 * BLOCK
ROWS = EB * BLOCK
GROUP = 64
EARLY = 2
ACROSS = (ROWS,)
PARTS = (ROWS // 2, ROWS // 2)
FLOOR = 2.0**-110
VMEM = pl.BlockSpec(memory_space=pltpu.VMEM)
SMEM = pl.BlockSpec(memory_space=pltpu.SMEM)
ANY = pl.BlockSpec(memory_space=pl.ANY)


def params():
    return pltpu.CompilerParams(vmem_limit_bytes=40 * 1024 * 1024)


def cost(flops, nbytes):
    return pl.CostEstimate(flops=flops, bytes_accessed=nbytes, transcendentals=0)


def parity():
    return lax.rem(lax.axis_index("grp") * lax.axis_size("blk") + lax.axis_index("blk"), 2)


def pick_kernel(members, capacity, ids, counts, source, *refs):
    picked, (blocks, id_list, count_list, sems) = refs[:members], refs[members:]
    own = lax.axis_index("blk")
    rows = blocks.shape[0] // 2
    parts = [pl.ds(n * rows, rows) for n in range(2)]
    pairs = [(ids, id_list), (counts, count_list)] + [(source.at[part], blocks.at[part]) for part in parts]
    copies = [pltpu.make_async_copy(here, there, sems.at[n]) for n, (here, there) in enumerate(pairs)]
    for n, copy in enumerate(copies):
        copy.start(priority=n % 2)
    for copy in copies:
        copy.wait()
    for k in range(members):
        reader = lax.rem(own + k, members)
        for j in range(capacity):
            start = pl.multiple_of(id_list[0, reader * capacity + j] * BLOCK, BLOCK)
            live = (j < count_list[0, reader]).astype(jnp.float32).astype(jnp.bfloat16)
            picked[k][j * BLOCK : (j + 1) * BLOCK] = blocks[pl.ds(start, BLOCK)] * live


def in_hbm(*arrays):
    return [pltpu.with_memory_space_constraint(x, pltpu.HBM) for x in arrays]


def pick(members, capacity, send_ids, send_counts, source):
    shape = (capacity * BLOCK, COLS)
    return pl.pallas_call(
        functools.partial(pick_kernel, members, capacity),
        out_shape=[pltpu.VMEM(shape, jnp.bfloat16)] * members,
        in_specs=[ANY] * 3,
        out_specs=[VMEM] * members,
        scratch_shapes=[
            pltpu.VMEM(source.shape, source.dtype),
            pltpu.SMEM(send_ids.shape, jnp.int32),
            pltpu.SMEM(send_counts.shape, jnp.int32),
            pltpu.SemaphoreType.DMA((4,)),
        ],
        compiler_params=params(),
        name="pick",
    )(*in_hbm(send_ids, send_counts, source))


def lanes_of(k, members):
    if k < EARLY:
        return k * CHUNK, (EARLY + k) * CHUNK
    return (EARLY + k) * CHUNK, (members + k) * CHUNK


def spread_kernel(members, capacity, quarters, slots_here, targets_here, weights, *refs):
    outs, (slots, targets, held, sems) = refs[:-4], refs[-4:]
    half = weights.shape[1] // 2
    parts = [held.at[:, pl.ds(n * half, half)] for n in range(2)]
    copies = [pltpu.make_async_copy(weights.at[:, pl.ds(n * half, half)], parts[n], sems.at[n]) for n in range(2)]
    lists = ((slots_here, slots), (targets_here, targets))
    lists = [pltpu.make_async_copy(here, there, sems.at[2 + n]) for n, (here, there) in enumerate(lists)]
    for copy in lists + copies:
        copy.start()
    for copy in lists:
        copy.wait()
    own = lax.axis_index("blk")
    tiles = weights.shape[0]
    count = len(quarters)
    slot = slots[...]
    sender = slot // capacity
    place = lax.rem(own - sender + members, members) * capacity + slot % capacity
    target = targets[...]
    rows = lax.broadcasted_iota(jnp.int32, (count * EB, tiles), 0)
    wanted = rows
    for n, (even, odd) in enumerate(quarters):
        wanted = jnp.where(rows // EB == n, rows % EB + jnp.where(parity() == 1, odd, even) * EB, wanted)
    hit = target == wanted
    table = jnp.concatenate(
        [
            (hit & (place == k * capacity + j)).astype(jnp.float32)
            for j in range(capacity)
            for k in range(members)
        ],
        axis=0,
    ).astype(jnp.bfloat16)
    side = members * count * EB
    left = lax.broadcasted_iota(jnp.int32, (side, CHUNK), 1) < BLOCK

    def step(part, first, c, _):
        x = part[:, pl.ds(pl.multiple_of(c * CHUNK, CHUNK), CHUNK)]
        c = c + first
        sums = jnp.dot(table, x, preferred_element_type=jnp.float32)
        one, two = sums[:side], sums[side:]
        halves = (
            jnp.where(left, one, pltpu.roll(two, BLOCK, 1)),
            jnp.where(left, pltpu.roll(one, BLOCK, 1), two),
        )
        for h, value in enumerate(halves):
            coarse = value.astype(jnp.bfloat16)
            fine = (value - coarse.astype(jnp.float32)).astype(jnp.bfloat16)
            row = pl.ds(pl.multiple_of((2 * c + h) * EB, EB), EB)
            for k in range(members):
                for n in range(count):
                    top = (k * count + n) * EB
                    for lanes, part in zip(lanes_of(k, members), (coarse, fine)):
                        outs[n][row, lanes : lanes + CHUNK] = part[top : top + EB]
        return 0

    each = half // CHUNK
    for n in range(2):
        copies[n].wait()
        lax.fori_loop(0, each, functools.partial(step, parts[n], n * each), 0, unroll=each)


def spread(members, capacity, quarters, slots, targets, weights):
    shape = (ROWS, 2 * members * CHUNK)
    tiles = weights.shape[0]
    return pl.pallas_call(
        functools.partial(spread_kernel, members, capacity, quarters),
        out_shape=[pltpu.VMEM(shape, jnp.bfloat16)] * len(quarters),
        in_specs=[ANY] * 3,
        out_specs=[VMEM] * len(quarters),
        scratch_shapes=[
            pltpu.VMEM(slots.shape, jnp.int32),
            pltpu.VMEM(targets.shape, jnp.int32),
            pltpu.VMEM(weights.shape, weights.dtype),
            pltpu.SemaphoreType.DMA((4,)),
        ],
        compiler_params=params(),
        cost_estimate=cost(2 * members * EB * len(quarters) * 2 * tiles * 8192, 6 * 2**20),
        name="spread",
    )(*in_hbm(slots, targets, weights))


def stacked(blocks, both):
    rows = blocks[0].shape[0]
    for half in range(2):
        for k, block in enumerate(blocks):
            start = (half * len(blocks) + k) * rows
            both[start : start + rows] = block[...]


def early_kernel(left, *refs):
    blocks, (sums, both) = refs[:-2], refs[-2:]
    stacked(blocks, both)
    sums[...] = jnp.dot(left[:, : both.shape[0]], both[...], preferred_element_type=jnp.float32)


def early(left, blocks):
    depth = 2 * EARLY * CHUNK
    return pl.pallas_call(
        early_kernel,
        out_shape=[pltpu.VMEM((ROWS, COLS), jnp.float32), pltpu.VMEM((depth, COLS), jnp.bfloat16)],
        in_specs=[VMEM] * (1 + len(blocks)),
        out_specs=[VMEM] * 2,
        compiler_params=params(),
        cost_estimate=cost(2 * ROWS * depth * COLS, 2 * 2**20),
        name="early",
    )(left, *blocks)


def coded(piece, message, powers):
    count = piece.shape[0]
    if count // GROUP < powers.shape[0]:
        powers[...] = jnp.zeros_like(powers)
    for g in range(count // GROUP):
        rows = piece[g * GROUP : (g + 1) * GROUP]
        most = jnp.maximum(jnp.max(jnp.abs(rows), axis=0, keepdims=True), FLOOR)
        power = jnp.floor(jnp.log2(most) + 0.001) + 1.0
        whole = jnp.round(rows * jnp.exp2(15.0 - power)).astype(jnp.int32)
        message[g * GROUP : (g + 1) * GROUP] = whole.astype(jnp.int16)
        powers[g : g + 1] = power.astype(jnp.int32)
    message[count : count + powers.shape[0]] = powers[...].astype(jnp.int16)


def product(left, first, later):
    both = jnp.concatenate([first[...], later[...]], axis=0)
    return jnp.dot(left, both, preferred_element_type=jnp.float32)


def across_kernel(parts, left, sums, *refs):
    blocks, refs = refs[: -2 * len(parts) - 1], refs[-2 * len(parts) - 1 :]
    messages, both, powers = refs[: len(parts)], refs[len(parts)], refs[len(parts) + 1 :]
    stacked(blocks, both)
    start = left.shape[1] - both.shape[0]
    piece = sums[...] + jnp.dot(left[:, start:], both[...], preferred_element_type=jnp.float32)
    first = 0
    for count, message, power in zip(parts, messages, powers):
        coded(piece[first : first + count], message, power)
        first += count


def scales(count):
    return max(count // GROUP, 16)


def message_of(count):
    return pltpu.VMEM((count + scales(count), COLS), jnp.int16)


def powers_of(count):
    return pltpu.VMEM((scales(count), COLS), jnp.int32)


def across_edge(parts, left, sums, blocks):
    depth = 2 * len(blocks) * CHUNK
    return pl.pallas_call(
        functools.partial(across_kernel, parts),
        out_shape=[message_of(count) for count in parts] + [pltpu.VMEM((depth, COLS), jnp.bfloat16)],
        in_specs=[VMEM] * (2 + len(blocks)),
        out_specs=[VMEM] * (len(parts) + 1),
        scratch_shapes=[powers_of(count) for count in parts],
        compiler_params=params(),
        cost_estimate=cost(2 * ROWS * depth * COLS, 2 * 2**20),
        name="across",
    )(left, sums, *blocks)


def chip_kernel(parts, left, first, later, *refs):
    start = 0
    for count, message, powers in zip(parts, refs[: len(parts)], refs[len(parts) :]):
        coded(product(left[start : start + count], first, later), message, powers)
        start += count


def chip_edge(parts, left, first, later):
    return pl.pallas_call(
        functools.partial(chip_kernel, parts),
        out_shape=[message_of(count) for count in parts],
        in_specs=[VMEM] * 3,
        out_specs=[VMEM] * len(parts),
        scratch_shapes=[powers_of(count) for count in parts],
        compiler_params=params(),
        cost_estimate=cost(2 * ROWS * left.shape[1] * COLS, 2 * 2**20),
        name="chip",
    )(left, first, later)


def middle_kernel(left_0, left_1, first, later, *outs):
    step = 256
    for left, out in zip((left_0, left_1), outs):
        for start in range(0, ROWS, step):
            out[start : start + step] = product(left[start : start + step], first, later)


def middle(left_0, left_1, first, later):
    return pl.pallas_call(
        middle_kernel,
        out_shape=[pltpu.VMEM((ROWS, COLS), jnp.float32)] * 2,
        in_specs=[VMEM] * 4,
        out_specs=[VMEM] * 2,
        compiler_params=params(),
        cost_estimate=cost(4 * ROWS * left_0.shape[1] * COLS, 4 * 2**20),
        name="middle",
    )(left_0, left_1, first, later)


def finish_kernel(across, low, parts, own, *refs):
    messages, (out, rows, sems) = refs[: len(parts)], refs[-3:]
    half = parity() if across else 1 - parity()
    high = low + sum(parts) // EB
    pitch = high - low + 8
    targets = rows.reshape(COLS // 128, EB, pitch, 128)
    some = EB // 2
    copies = []
    for first in range(0, EB, some):
        i = low
        for count, message in zip(parts, messages):
            scale = jnp.exp2(message[count : count + scales(count)].astype(jnp.float32) - 15.0)
            for at in range(0, count, EB):
                g = at // GROUP
                value = message[at : at + EB].astype(jnp.float32)[first : first + some]
                value = own[i * EB + first : i * EB + first + some] + value * scale[g : g + 1]
                for n in range(COLS // 128):
                    place = pl.ds(first * pitch + i - low, some, stride=pitch)
                    rows[n, place] = value[:, n * 128 : (n + 1) * 128]
                i += 1
        for n in range(COLS // 128):
            here = targets.at[n, pl.ds(first, some), pl.ds(0, high - low)]
            there = out.at[pl.ds(half * EB + first, some), pl.ds(low, high - low), pl.ds(n * 128, 128)]
            copies.append(pltpu.make_async_copy(here, there, sems.at[len(copies)]))
            copies[-1].start()
    for copy in copies:
        copy.wait()


def finish(across, low, parts, own, messages, out=None):
    given = [] if out is None else [out]
    pitch = sum(parts) // EB + 8
    return pl.pallas_call(
        functools.partial(finish_kernel, across, low, parts),
        out_shape=jax.ShapeDtypeStruct((2 * EB, BLOCK, COLS), jnp.float32),
        in_specs=[VMEM] * (1 + len(parts)) + [ANY] * len(given),
        out_specs=ANY,
        scratch_shapes=[
            pltpu.VMEM((COLS // 128, EB * pitch, 128), jnp.float32),
            pltpu.SemaphoreType.DMA((2 * COLS // 128,)),
        ],
        input_output_aliases={} if out is None else {1 + len(parts): 0},
        compiler_params=params(),
        cost_estimate=cost(3 * sum(parts) * COLS, 2 * 2**20 * sum(parts) // ROWS),
        name="finish",
    )(own, *messages, *given)


def passed_along(shard, axis, by):
    count = lax.axis_size(axis)
    return lax.ppermute(shard, axis, [(i, (i + by) % count) for i in range(count)])


def ring_swap(shard, across):
    axes = ("grp", "blk")
    count = lax.axis_size(axes)
    if across:
        return lax.ppermute(shard, axes, [(i, (i + (1 if i % 2 else -1)) % count) for i in range(count)])
    return lax.ppermute(shard, axes, [(i, i ^ 1) for i in range(count)])


def body(source, send_ids, send_counts, tile_slot, tile_target, tile_weights):
    members = lax.axis_size("blk")
    capacity = send_ids.shape[1] // members
    picked = pick(members, capacity, send_ids, send_counts, source)
    tiles = (tile_slot, tile_target)
    blocks = [picked[0]] + [passed_along(picked[k], "blk", k) for k in range(1, members)]
    (left_across,) = spread(members, capacity, ((0, 3),), *tiles, tile_weights)
    sums, first = early(left_across, blocks[:EARLY])
    message_across, later = across_edge(ACROSS, left_across, sums, blocks[EARLY:])
    message_across = ring_swap(message_across, True)
    tiles, later = lax.optimization_barrier((tiles, later))
    left_chip, *own_left = spread(members, capacity, ((3, 0), (1, 2), (2, 1)), *tiles, tile_weights)
    own_across, own_chip = middle(*own_left, first, later)
    own_across, left_chip = lax.optimization_barrier((own_across, left_chip))
    messages_chip = [ring_swap(message, False) for message in chip_edge(PARTS, left_chip, first, later)]
    out = finish(False, 0, PARTS, own_chip, messages_chip)
    out = finish(True, 0, ACROSS, own_across, [message_across], out)
    return out.reshape(2 * ROWS, COLS)


def solution(mesh):
    spec = P(("grp", "blk"), None)
    return jax.shard_map(body, mesh=mesh, in_specs=(spec,) * 6, out_specs=spec, check_vma=False)
```

```python
import functools

import jax
import jax.numpy as jnp
from jax import lax
from jax.experimental import pallas as pl
from jax.experimental.pallas import tpu as pltpu
from jax.sharding import PartitionSpec as P

COLS = 256
BLOCK = 64
EB = 16
CHUNK = 2 * BLOCK
ROWS = EB * BLOCK
GROUP = 128
EARLY = 2
ACROSS = (ROWS,)
PARTS = (ROWS // 2, ROWS // 2)
FLOOR = 2.0**-110
VMEM = pl.BlockSpec(memory_space=pltpu.VMEM)
SMEM = pl.BlockSpec(memory_space=pltpu.SMEM)
ANY = pl.BlockSpec(memory_space=pl.ANY)


def params():
    return pltpu.CompilerParams(vmem_limit_bytes=40 * 1024 * 1024)


def cost(flops, nbytes):
    return pl.CostEstimate(flops=flops, bytes_accessed=nbytes, transcendentals=0)


def parity():
    return lax.rem(lax.axis_index("grp") * lax.axis_size("blk") + lax.axis_index("blk"), 2)


def pick_kernel(members, capacity, ids, counts, source, slots, targets, *refs):
    picked, (slot_list, target_list, blocks, id_list, count_list, sems) = refs[:members], refs[members:]
    own = lax.axis_index("blk")
    pairs = (
        (ids, id_list),
        (counts, count_list),
        (source, blocks),
        (slots, slot_list),
        (targets, target_list),
    )
    copies = [pltpu.make_async_copy(here, there, sems.at[n]) for n, (here, there) in enumerate(pairs)]
    for copy in copies:
        copy.start()
    for copy in copies[:3]:
        copy.wait()
    for k in range(members):
        reader = lax.rem(own + k, members)
        for j in range(capacity):
            start = pl.multiple_of(id_list[0, reader * capacity + j] * BLOCK, BLOCK)
            live = (j < count_list[0, reader]).astype(jnp.float32).astype(jnp.bfloat16)
            picked[k][j * BLOCK : (j + 1) * BLOCK] = blocks[pl.ds(start, BLOCK)] * live
    for copy in copies[3:]:
        copy.wait()


def in_hbm(*arrays):
    return [pltpu.with_memory_space_constraint(x, pltpu.HBM) for x in arrays]


def pick(members, capacity, send_ids, send_counts, source, slots, targets):
    shape = (capacity * BLOCK, COLS)
    results = pl.pallas_call(
        functools.partial(pick_kernel, members, capacity),
        out_shape=[pltpu.VMEM(shape, jnp.bfloat16)] * members
        + [pltpu.VMEM(slots.shape, jnp.int32), pltpu.VMEM(targets.shape, jnp.int32)],
        in_specs=[ANY] * 5,
        out_specs=[VMEM] * (members + 2),
        scratch_shapes=[
            pltpu.VMEM(source.shape, source.dtype),
            pltpu.SMEM(send_ids.shape, jnp.int32),
            pltpu.SMEM(send_counts.shape, jnp.int32),
            pltpu.SemaphoreType.DMA((5,)),
        ],
        compiler_params=params(),
        name="pick",
    )(*in_hbm(send_ids, send_counts, source, slots, targets))
    return results[:members], results[members:]


def lanes_of(k, members):
    if k < EARLY:
        return k * CHUNK, (EARLY + k) * CHUNK
    return (EARLY + k) * CHUNK, (members + k) * CHUNK


def spread_kernel(members, capacity, quarters, slots, targets, weights, *refs):
    outs, (held, sems) = refs[:-2], refs[-2:]
    half = weights.shape[1] // 2
    parts = [held.at[:, pl.ds(n * half, half)] for n in range(2)]
    copies = [pltpu.make_async_copy(weights.at[:, pl.ds(n * half, half)], parts[n], sems.at[n]) for n in range(2)]
    for copy in copies:
        copy.start()
    own = lax.axis_index("blk")
    tiles = weights.shape[0]
    count = len(quarters)
    slot = slots[...]
    sender = slot // capacity
    place = lax.rem(own - sender + members, members) * capacity + slot % capacity
    target = targets[...]
    rows = lax.broadcasted_iota(jnp.int32, (count * EB, tiles), 0)
    wanted = rows
    for n, (even, odd) in enumerate(quarters):
        wanted = jnp.where(rows // EB == n, rows % EB + jnp.where(parity() == 1, odd, even) * EB, wanted)
    hit = target == wanted
    table = jnp.concatenate(
        [
            (hit & (place == k * capacity + j)).astype(jnp.float32)
            for j in range(capacity)
            for k in range(members)
        ],
        axis=0,
    ).astype(jnp.bfloat16)
    side = members * count * EB
    left = lax.broadcasted_iota(jnp.int32, (side, CHUNK), 1) < BLOCK

    def step(part, first, c, _):
        x = part[:, pl.ds(pl.multiple_of(c * CHUNK, CHUNK), CHUNK)]
        c = c + first
        sums = jnp.dot(table, x, preferred_element_type=jnp.float32)
        one, two = sums[:side], sums[side:]
        halves = (
            jnp.where(left, one, pltpu.roll(two, BLOCK, 1)),
            jnp.where(left, pltpu.roll(one, BLOCK, 1), two),
        )
        for h, value in enumerate(halves):
            coarse = value.astype(jnp.bfloat16)
            fine = (value - coarse.astype(jnp.float32)).astype(jnp.bfloat16)
            row = pl.ds(pl.multiple_of((2 * c + h) * EB, EB), EB)
            for k in range(members):
                for n in range(count):
                    top = (k * count + n) * EB
                    for lanes, part in zip(lanes_of(k, members), (coarse, fine)):
                        outs[n][row, lanes : lanes + CHUNK] = part[top : top + EB]
        return 0

    each = half // CHUNK
    for n in range(2):
        copies[n].wait()
        lax.fori_loop(0, each, functools.partial(step, parts[n], n * each), 0, unroll=each)


def spread(members, capacity, quarters, slots, targets, weights):
    shape = (ROWS, 2 * members * CHUNK)
    tiles = weights.shape[0]
    return pl.pallas_call(
        functools.partial(spread_kernel, members, capacity, quarters),
        out_shape=[pltpu.VMEM(shape, jnp.bfloat16)] * len(quarters),
        in_specs=[VMEM] * 2 + [ANY],
        out_specs=[VMEM] * len(quarters),
        scratch_shapes=[
            pltpu.VMEM(weights.shape, weights.dtype),
            pltpu.SemaphoreType.DMA((2,)),
        ],
        compiler_params=params(),
        cost_estimate=cost(2 * members * EB * len(quarters) * 2 * tiles * 8192, 6 * 2**20),
        name="spread",
    )(slots, targets, *in_hbm(weights))


def stacked(blocks, both):
    rows = blocks[0].shape[0]
    for half in range(2):
        for k, block in enumerate(blocks):
            start = (half * len(blocks) + k) * rows
            both[start : start + rows] = block[...]


def early_kernel(left, *refs):
    blocks, (sums, both) = refs[:-2], refs[-2:]
    stacked(blocks, both)
    sums[...] = jnp.dot(left[:, : both.shape[0]], both[...], preferred_element_type=jnp.float32)


def early(left, blocks):
    depth = 2 * EARLY * CHUNK
    return pl.pallas_call(
        early_kernel,
        out_shape=[pltpu.VMEM((ROWS, COLS), jnp.float32), pltpu.VMEM((depth, COLS), jnp.bfloat16)],
        in_specs=[VMEM] * (1 + len(blocks)),
        out_specs=[VMEM] * 2,
        compiler_params=params(),
        cost_estimate=cost(2 * ROWS * depth * COLS, 2 * 2**20),
        name="early",
    )(left, *blocks)


def coded(piece, message, powers):
    count = piece.shape[0]
    if count // GROUP < powers.shape[0]:
        powers[...] = jnp.zeros_like(powers)
    for g in range(count // GROUP):
        rows = piece[g * GROUP : (g + 1) * GROUP]
        most = jnp.maximum(jnp.max(jnp.abs(rows), axis=0, keepdims=True), FLOOR)
        power = jnp.floor(jnp.log2(most) + 0.001) + 1.0
        whole = jnp.round(rows * jnp.exp2(15.0 - power)).astype(jnp.int32)
        message[g * GROUP : (g + 1) * GROUP] = whole.astype(jnp.int16)
        powers[g : g + 1] = power.astype(jnp.int32)
    message[count : count + powers.shape[0]] = powers[...].astype(jnp.int16)


def product(left, first, later):
    both = jnp.concatenate([first[...], later[...]], axis=0)
    return jnp.dot(left, both, preferred_element_type=jnp.float32)


def across_kernel(parts, left, sums, *refs):
    blocks, refs = refs[: -2 * len(parts) - 1], refs[-2 * len(parts) - 1 :]
    messages, both, powers = refs[: len(parts)], refs[len(parts)], refs[len(parts) + 1 :]
    stacked(blocks, both)
    start = left.shape[1] - both.shape[0]
    piece = sums[...] + jnp.dot(left[:, start:], both[...], preferred_element_type=jnp.float32)
    first = 0
    for count, message, power in zip(parts, messages, powers):
        coded(piece[first : first + count], message, power)
        first += count


def scales(count):
    return max(count // GROUP, 16)


def message_of(count):
    return pltpu.VMEM((count + scales(count), COLS), jnp.int16)


def powers_of(count):
    return pltpu.VMEM((scales(count), COLS), jnp.int32)


def across_edge(parts, left, sums, blocks):
    depth = 2 * len(blocks) * CHUNK
    return pl.pallas_call(
        functools.partial(across_kernel, parts),
        out_shape=[message_of(count) for count in parts] + [pltpu.VMEM((depth, COLS), jnp.bfloat16)],
        in_specs=[VMEM] * (2 + len(blocks)),
        out_specs=[VMEM] * (len(parts) + 1),
        scratch_shapes=[powers_of(count) for count in parts],
        compiler_params=params(),
        cost_estimate=cost(2 * ROWS * depth * COLS, 2 * 2**20),
        name="across",
    )(left, sums, *blocks)


def chip_kernel(parts, left, first, later, *refs):
    start = 0
    for count, message, powers in zip(parts, refs[: len(parts)], refs[len(parts) :]):
        coded(product(left[start : start + count], first, later), message, powers)
        start += count


def chip_edge(parts, left, first, later):
    return pl.pallas_call(
        functools.partial(chip_kernel, parts),
        out_shape=[message_of(count) for count in parts],
        in_specs=[VMEM] * 3,
        out_specs=[VMEM] * len(parts),
        scratch_shapes=[powers_of(count) for count in parts],
        compiler_params=params(),
        cost_estimate=cost(2 * ROWS * left.shape[1] * COLS, 2 * 2**20),
        name="chip",
    )(left, first, later)


def middle_kernel(left_0, left_1, first, later, *outs):
    step = 256
    for left, out in zip((left_0, left_1), outs):
        for start in range(0, ROWS, step):
            out[start : start + step] = product(left[start : start + step], first, later)


def middle(left_0, left_1, first, later):
    return pl.pallas_call(
        middle_kernel,
        out_shape=[pltpu.VMEM((ROWS, COLS), jnp.float32)] * 2,
        in_specs=[VMEM] * 4,
        out_specs=[VMEM] * 2,
        compiler_params=params(),
        cost_estimate=cost(4 * ROWS * left_0.shape[1] * COLS, 4 * 2**20),
        name="middle",
    )(left_0, left_1, first, later)


def finish_kernel(across, low, parts, own, *refs):
    messages, (out, rows, sems) = refs[: len(parts)], refs[-3:]
    half = parity() if across else 1 - parity()
    high = low + sum(parts) // EB
    pitch = high - low + 8
    targets = rows.reshape(COLS // 128, EB, pitch, 128)
    some = EB // 2
    copies = []
    for first in range(0, EB, some):
        i = low
        for count, message in zip(parts, messages):
            scale = jnp.exp2(message[count : count + scales(count)].astype(jnp.float32) - 15.0)
            for at in range(0, count, EB):
                g = at // GROUP
                value = message[at : at + EB].astype(jnp.float32)[first : first + some]
                value = own[i * EB + first : i * EB + first + some] + value * scale[g : g + 1]
                for n in range(COLS // 128):
                    place = pl.ds(first * pitch + i - low, some, stride=pitch)
                    rows[n, place] = value[:, n * 128 : (n + 1) * 128]
                i += 1
        for n in range(COLS // 128):
            here = targets.at[n, pl.ds(first, some), pl.ds(0, high - low)]
            there = out.at[pl.ds(half * EB + first, some), pl.ds(low, high - low), pl.ds(n * 128, 128)]
            copies.append(pltpu.make_async_copy(here, there, sems.at[len(copies)]))
            copies[-1].start()
    for copy in copies:
        copy.wait()


def finish(across, low, parts, own, messages, out=None):
    given = [] if out is None else [out]
    pitch = sum(parts) // EB + 8
    return pl.pallas_call(
        functools.partial(finish_kernel, across, low, parts),
        out_shape=jax.ShapeDtypeStruct((2 * EB, BLOCK, COLS), jnp.float32),
        in_specs=[VMEM] * (1 + len(parts)) + [ANY] * len(given),
        out_specs=ANY,
        scratch_shapes=[
            pltpu.VMEM((COLS // 128, EB * pitch, 128), jnp.float32),
            pltpu.SemaphoreType.DMA((2 * COLS // 128,)),
        ],
        input_output_aliases={} if out is None else {1 + len(parts): 0},
        compiler_params=params(),
        cost_estimate=cost(3 * sum(parts) * COLS, 2 * 2**20 * sum(parts) // ROWS),
        name="finish",
    )(own, *messages, *given)


def passed_along(shard, axis, by):
    count = lax.axis_size(axis)
    return lax.ppermute(shard, axis, [(i, (i + by) % count) for i in range(count)])


def ring_swap(shard, across):
    axes = ("grp", "blk")
    count = lax.axis_size(axes)
    if across:
        return lax.ppermute(shard, axes, [(i, (i + (1 if i % 2 else -1)) % count) for i in range(count)])
    return lax.ppermute(shard, axes, [(i, i ^ 1) for i in range(count)])


def body(source, send_ids, send_counts, tile_slot, tile_target, tile_weights):
    members = lax.axis_size("blk")
    capacity = send_ids.shape[1] // members
    picked, tiles = pick(
        members, capacity, send_ids, send_counts, source, tile_slot, tile_target
    )
    blocks = [picked[0]] + [passed_along(picked[k], "blk", k) for k in range(1, members)]
    (left_across,) = spread(members, capacity, ((0, 3),), *tiles, tile_weights)
    sums, first = early(left_across, blocks[:EARLY])
    message_across, later = across_edge(ACROSS, left_across, sums, blocks[EARLY:])
    message_across = ring_swap(message_across, True)
    tiles, later = lax.optimization_barrier((tiles, later))
    left_chip, *own_left = spread(members, capacity, ((3, 0), (1, 2), (2, 1)), *tiles, tile_weights)
    messages_chip = [ring_swap(message, False) for message in chip_edge(PARTS, left_chip, first, later)]
    own_across, own_chip = middle(*own_left, first, later)
    out = finish(False, 0, PARTS, own_chip, messages_chip)
    out = finish(True, 0, ACROSS, own_across, [message_across], out)
    return out.reshape(2 * ROWS, COLS)


def solution(mesh):
    spec = P(("grp", "blk"), None)
    return jax.shard_map(body, mesh=mesh, in_specs=(spec,) * 6, out_specs=spec, check_vma=False)
```
